256 devices in a mesh: polar: 16 (over y, x), azimuth: 16 (over z, core).
Axes of the slice: x: 4, y: 4, z: 8, core: 2. Of those that a mesh axis runs over, the one named last changes fastest.
Arguments:
- grid_state: bfloat16 [128, 1024, 640], P('polar', 'azimuth'), may hold values from -6 to 6
- filter_taps: bfloat16 [128, 9, 4, 129], P('polar'), may hold values from -0.59765625 to 0.59765625
- support_start: int32 [128], P('polar'), may hold values from -64 to 64, as said below
- support_count: int32 [128], P('polar'), may hold values from 1 to 129
- filter_mix: bfloat16 [2, 9, 640], replicated, may hold values from -2 to 2
- w_in: bfloat16 [2, 640, 1280], replicated, may hold values from -0.25 to 0.25
- w_out: bfloat16 [2, 1280, 640], replicated, may hold values from -0.15625 to 0.15625
Outputs:
- next_state: bfloat16 [128, 1024, 640], P('polar', 'azimuth')
The draws below stay inside these ranges and needn't reach their ends.
Inputs may be any that keep to these rules, and one draw needn't show every extreme that they name: support_start[i] + support_count[i] - 1 <= 64; support is widest near the poles.
All inputs are finite; a program needn't handle non-finite values.
Results may differ from the reference program's by a relative error of at most 0.006.
Values may be sent and summed in bfloat16 or wider, within the bound.
A program may use at most 64 MiB of HBM per device.

```python
import jax
import jax.numpy as jnp
from jax import lax

C = 640
HID = 1280
FILTERS = 9
ROWS = 4
LAYERS = 2
LON_DEV = 64
HALF = 64
TAPS = 129
NLAT = 128
NLON = 1024


def support_tables(key):
    latitude = jnp.arange(NLAT, dtype=jnp.int32)
    polar_gap = jnp.minimum(latitude, NLAT - 1 - latitude)
    widest = TAPS // (polar_gap + 1)
    jitter = jax.random.randint(jax.random.fold_in(key, 11), (NLAT,), 0, 9, dtype=jnp.int32)
    counts = jnp.clip(widest + jitter, 1, TAPS)
    middle = latitude == NLAT // 2
    counts = jnp.where(middle, 1, counts)
    slack = TAPS - counts
    raw_shift = jax.random.randint(jax.random.fold_in(key, 12), (NLAT,), 0, 1048576, dtype=jnp.int32)
    starts = raw_shift % (slack + 1) - HALF
    starts = jnp.where(middle, HALF, starts)
    return (starts.astype(jnp.int32), counts.astype(jnp.int32))


def draw_support_start(key, part):
    return support_tables(key)[0]


def draw_support_count(key, part):
    return support_tables(key)[1]


def level_of(key, dims, pieces, smallest, largest):
    def one(dim, shards_of):
        steps = jax.random.uniform(jax.random.fold_in(jax.random.fold_in(key, 6), dim), (shards_of,), jnp.float32, smallest / len(pieces), largest / len(pieces))
        return jnp.repeat(jnp.exp(steps), dims[dim] // shards_of).reshape((-1,) + (1,) * (len(dims) - dim - 1))

    level = one(*pieces[0])
    for cut in pieces[1:]:
        level = level * one(*cut)
    return level


def bell_draw(rng, extent, scale, limit, pieces=(), kind=jnp.bfloat16):
    gain = level_of(rng, extent, pieces, -0.22, 0.18) if pieces else 1.0
    entries = jax.random.normal(rng, extent, jnp.float32) * scale * gain
    return jnp.minimum(jnp.maximum(entries, -limit), limit).astype(kind)


def setup_inputs(seed: int = 0) -> dict:
    arg_keys = jax.random.split(jax.random.key(seed), 8)
    grid_state = bell_draw(arg_keys[0], (NLAT, NLON, C), 1.0, 6.0, ((0, 16), (1, 16)))
    filter_taps = bell_draw(arg_keys[1], (NLAT, FILTERS, ROWS, TAPS), 0.1, 0.59765625, ((0, 16),))
    support_start = draw_support_start(jax.random.fold_in(arg_keys[7], 71), 0)
    support_count = draw_support_count(jax.random.fold_in(arg_keys[7], 71), 0)
    filter_mix = bell_draw(arg_keys[4], (LAYERS, FILTERS, C), 0.35, 2.0)
    w_in = bell_draw(arg_keys[5], (LAYERS, C, HID), C ** -0.5, 0.25)
    w_out = bell_draw(arg_keys[6], (LAYERS, HID, C), HID ** -0.5, 0.15625)
    return dict(grid_state=grid_state, filter_taps=filter_taps, support_start=support_start, support_count=support_count, filter_mix=filter_mix, w_in=w_in, w_out=w_out)


def tap_bands(filter_taps, support_start, support_count, reach):
    tap_count = filter_taps.shape[-1]
    offsets = jnp.arange(tap_count, dtype=jnp.int32) - reach
    inside = (offsets[None, :] >= support_start[:, None]) & (offsets[None, :] < (support_start + support_count)[:, None])
    masked = jnp.where(inside[:, None, None, :], filter_taps.astype(jnp.float32), jnp.float32(0.0))
    column = jnp.arange(reach, dtype=jnp.int32)[:, None]
    window = jnp.arange(3 * reach, dtype=jnp.int32)[None, :]
    onehot = ((window - column)[:, :, None] == jnp.arange(tap_count, dtype=jnp.int32)[None, None, :]).astype(jnp.float32)
    return jnp.einsum("akrt,jwt->akjrw", masked, onehot).astype(jnp.bfloat16)


def block_windows(rows, reach):
    blocks = rows.shape[1] // reach
    extended = jnp.concatenate([rows[:, -reach:], rows, rows[:, :reach]], axis=1)
    extended = extended.reshape(rows.shape[0], blocks + 2, reach, rows.shape[2])
    return jnp.concatenate([extended[:, :blocks], extended[:, 1:blocks + 1], extended[:, 2:]], axis=2)


def channel_mlp(act, field, first, second):
    flat = act.reshape(-1, act.shape[-1])
    hidden = jax.nn.gelu(jnp.dot(flat, first, preferred_element_type=jnp.float32), approximate=False).astype(jnp.bfloat16)
    update = jnp.dot(hidden, second, preferred_element_type=jnp.float32)
    return (field.astype(jnp.float32) + update.reshape(field.shape)).astype(jnp.bfloat16)


def reference(grid_state, filter_taps, support_start, support_count, filter_mix, w_in, w_out):
    bands = tap_bands(filter_taps, support_start, support_count, LON_DEV)
    field = grid_state
    for layer_no in range(LAYERS):
        padded = jnp.pad(field, ((2, 1), (0, 0), (0, 0)))
        mix_row = filter_mix[layer_no].astype(jnp.float32)

        def one_latitude(lat_index):
            rows = lax.dynamic_slice_in_dim(padded, lat_index, 4, 0)
            windows = block_windows(rows, LON_DEV).astype(jnp.float32)
            band_rows = lax.dynamic_index_in_dim(bands, lat_index, 0, keepdims=False).astype(jnp.float32)
            conv = jnp.einsum("kjrw,rbwc->kbjc", band_rows, windows)
            mixed = jnp.einsum("kbjc,kc->bjc", conv, mix_row)
            return jax.nn.gelu(mixed, approximate=False).astype(jnp.bfloat16).reshape(NLON, C)

        act = lax.map(one_latitude, jnp.arange(NLAT, dtype=jnp.int32))
        field = channel_mlp(act, field, w_in[layer_no], w_out[layer_no])
    return field
```

```python
import functools

import jax
import jax.numpy as jnp
from jax import lax
from jax.experimental import pallas as pl
from jax.experimental.pallas import tpu as pltpu
from jax.sharding import PartitionSpec as P

F32 = jnp.float32
BF16 = jnp.bfloat16
MESH = pl.DeviceIdType.MESH
CHUNKS = ((0, 256), (256, 256), (512, 128))
NAMES = (
    "z6", "z0", "z4", "z1", "pairA", "pairB",
    "down", "up", "sdown", "sup", "fdown", "fup",
)


def gelu(x):
    return 0.5 * x * (1.0 + lax.erf(x * 0.7071067811865476))


def body(
    n_polar, n_azimuth,
    grid, taps, start, count, mix, w_in, w_out, out,
    f1, fz, ab, cc, w1, w2, src, mab, mcc, part, act, mixf,
    send_sem, recv_sem, local_sem,
):
    p = lax.axis_index("polar")
    a = lax.axis_index("azimuth")
    h = lax.rem(a, 2)
    pair = a + 1 - 2 * h
    zside = lax.rem(a + n_azimuth - 1 + 2 * h, n_azimuth)
    has_low = p > 0
    has_high = p < n_polar - 1
    own = pl.ds(pl.multiple_of(h * 64, 64), 64)

    barrier = pltpu.get_barrier_semaphore()
    for peer in (pair, zside):
        pl.semaphore_signal(barrier, inc=1, device_id=(p, peer), device_id_type=MESH)

    @pl.when(has_low)
    def _():
        pl.semaphore_signal(barrier, inc=1, device_id=(p - 1, a), device_id_type=MESH)

    @pl.when(has_high)
    def _():
        pl.semaphore_signal(barrier, inc=1, device_id=(p + 1, a), device_id_type=MESH)

    def field_rows(layer, row, rows):
        if layer == 0:
            return grid.at[pl.ds(row, rows)]
        return f1.at[layer, pl.ds(row + 2, rows), own]

    def transfer(layer, name):
        up_p, down_p = p + 1, p - 1
        if name[0] == "z":
            row = int(name[1])
            rows = 3 if row == 1 else (1 if row == 0 else 2)
            return (field_rows(layer, row, rows), fz.at[layer, pl.ds(row + 2, rows)], (p, zside), None, None)
        if name[:4] == "pair":
            row = 4 if name == "pairA" else 0
            return (field_rows(layer, row, 4), f1.at[layer, pl.ds(row + 2, 4), own], (p, pair), None, None)
        if name == "down":
            return (field_rows(layer, 6, 2), f1.at[layer, pl.ds(0, 2), own], (up_p, a), has_high, has_low)
        if name == "up":
            return (field_rows(layer, 0, 1), f1.at[layer, pl.ds(10, 1), own], (down_p, a), has_low, has_high)
        if name == "sdown":
            return (fz.at[layer, pl.ds(8, 2)], fz.at[layer, pl.ds(0, 2)], (up_p, a), has_high, has_low)
        if name == "sup":
            return (fz.at[layer, pl.ds(2, 1)], fz.at[layer, pl.ds(10, 1)], (down_p, a), has_low, has_high)
        if name == "fdown":
            return (f1.at[layer, pl.ds(0, 2), own], f1.at[layer, pl.ds(0, 2), own], (p, pair), has_low, has_low)
        return (f1.at[layer, pl.ds(10, 1), own], f1.at[layer, pl.ds(10, 1), own], (p, pair), has_high, has_high)

    def act_on(layer, name, what):
        source, target, device, sends, receives = transfer(layer, name)
        number = layer * len(NAMES) + NAMES.index(name)
        copy = pltpu.make_async_remote_copy(
            src_ref=source, dst_ref=target, send_sem=send_sem.at[number],
            recv_sem=recv_sem.at[number], device_id=device, device_id_type=MESH,
        )
        run = {"start": copy.start, "recv": copy.wait_recv, "sent": copy.wait_send}[what]
        when = receives if what == "recv" else sends
        if when is None:
            run()
        else:
            pl.when(when)(run)

    def begin(layer, *names):
        for name in names:
            act_on(layer, name, "start")

    def arrived(layer, *names):
        for name in names:
            act_on(layer, name, "recv")

    local = [
        pltpu.make_async_copy(grid, f1.at[0, pl.ds(2, 8), own], local_sem.at[0]),
        pltpu.make_async_copy(w_in.at[0], w1.at[0], local_sem.at[1]),
        pltpu.make_async_copy(w_out.at[0], w2.at[0], local_sem.at[2]),
        pltpu.make_async_copy(w_in.at[1], w1.at[1], local_sem.at[3]),
        pltpu.make_async_copy(w_out.at[1], w2.at[1], local_sem.at[4]),
    ]
    local[0].start()

    pl.semaphore_wait(barrier, 2 + has_low.astype(jnp.int32) + has_high.astype(jnp.int32))

    begin(0, "z6", "down", "pairA", "up", "z0", "pairB", "z4", "z1")
    for copy in local[1:]:
        copy.start()

    @pl.when(p == 0)
    def _():
        for layer in range(2):
            f1[layer, 0:2] = jnp.zeros((2, 128, 640), BF16)
            fz[layer, 0:2] = jnp.zeros((2, 64, 640), BF16)

    @pl.when(p == n_polar - 1)
    def _():
        for layer in range(2):
            f1[layer, 10:11] = jnp.zeros((1, 128, 640), BF16)
            fz[layer, 10:11] = jnp.zeros((1, 64, 640), BF16)

    for layer in range(2):
        mixf[layer, 0:9] = mix[layer].astype(F32)

    row64 = lax.broadcasted_iota(jnp.int32, (64, 128), 0)
    lane64 = lax.broadcasted_iota(jnp.int32, (64, 128), 1)
    tap_ab = 64 * (1 - h) + lane64 - row64
    mab[...] = jnp.where((tap_ab >= 0) & (tap_ab <= 128), 1.0, 0.0).astype(F32)
    tap_cc = 128 * h + (lane64 & 63) - row64
    mcc[...] = jnp.where((tap_cc >= 0) & (tap_cc <= 128), 1.0, 0.0).astype(F32)

    offset = lax.broadcasted_iota(jnp.int32, (4, 129), 1) - 64
    lane4 = lax.broadcasted_iota(jnp.int32, (4, 128), 1)
    first = lane4 == 0
    even = ((h == 0) & (lane4 < 64)) | ((h == 1) & (first | (lane4 > 64)))

    def sources(n, carry):
        i, k = n // 9, lax.rem(n, 9)
        inside = (offset >= start[i]) & (offset < start[i] + count[i])
        v = jnp.where(inside, taps[i, k].astype(F32), 0.0)
        low = v[:, 0:128]
        last = jnp.where(first, jnp.broadcast_to(v[:, 128:129], (4, 128)), low)
        v_ab = jnp.where(h == 0, pltpu.roll(last, 64, 1), low)
        v_cc = jnp.where(h == 0, low, last)
        other = pltpu.roll(v_cc, 64, 1)
        odd = jnp.concatenate([other[1:4], other[0:1]], axis=0)
        src[n, 0:4] = v_ab
        src[n, 4:8] = jnp.where(even, v_cc, odd)
        return carry

    lax.fori_loop(0, 72, sources, 0)

    def band(n, row, mask):
        base = jnp.broadcast_to(src[n, row : row + 1, :], (8, 128))
        base = pltpu.roll(base, 0, 1, stride=1, stride_axis=0)
        tiles = [base] + [pltpu.roll(base, 8 * j, 1) for j in range(1, 8)]
        return (jnp.concatenate(tiles, axis=0) * mask[...]).astype(BF16)

    def build(n, carry):
        i, k = n // 9, lax.rem(n, 9)
        rows = pl.ds(pl.multiple_of(k * 64, 64), 64)
        for r in range(4):
            ab[i, rows, 128 * r : 128 * r + 128] = band(n, r, mab)
        for r in range(2):
            cc[i, rows, 128 * r : 128 * r + 128] = band(n, 4 + 2 * r, mcc)
        return carry

    lax.fori_loop(0, 72, build, 0)

    def mixed(layer, r, c0, cw):
        total = r[0:64] * mixf[layer, 0:1, c0 : c0 + cw]
        for k in range(1, 9):
            total += r[64 * k : 64 * k + 64] * mixf[layer, k : k + 1, c0 : c0 + cw]
        return total

    def near(layer, lo, hi):
        def one(i, carry):
            rows = pl.ds(pl.multiple_of(i * 64, 64), 64)
            for c0, cw in CHUNKS:
                window = f1[layer, pl.ds(i, 4), :, c0 : c0 + cw].reshape(512, cw)
                r = jnp.dot(ab[i], window, preferred_element_type=F32)
                part[rows, c0 : c0 + cw] = mixed(layer, r, c0, cw)
            return carry

        lax.fori_loop(lo, hi, one, 0)

    def far(layer, lo, hi):
        def one(i, carry):
            rows = pl.ds(pl.multiple_of(i * 64, 64), 64)
            for c0, cw in CHUNKS:
                window = fz[layer, pl.ds(i, 4), :, c0 : c0 + cw].reshape(256, cw)
                r = jnp.dot(cc[i], window, preferred_element_type=F32)
                total = part[rows, c0 : c0 + cw] + mixed(layer, r, c0, cw)
                act[rows, c0 : c0 + cw] = gelu(total).astype(BF16)
            return carry

        lax.fori_loop(lo, hi, one, 0)

    def mlp(layer, row):
        hidden = jnp.dot(act[row * 64 : row * 64 + 256], w1[layer], preferred_element_type=F32)
        hidden = gelu(hidden).astype(BF16)
        update = jnp.dot(hidden, w2[layer], preferred_element_type=F32)
        field = f1[layer, row + 2 : row + 6, own, :].astype(F32)
        result = (field + update.reshape(4, 64, 640)).astype(BF16)
        if layer == 0:
            f1[1, row + 2 : row + 6, own, :] = result
        else:
            out[row : row + 4] = result

    arrived(0, "z6", "z0")
    begin(0, "sdown", "sup")
    local[0].wait()
    arrived(0, "pairA", "pairB")
    near(0, 4, 7)
    arrived(0, "down", "up")
    begin(0, "fdown", "fup")
    near(0, 2, 4)
    arrived(0, "fdown", "fup")
    near(0, 7, 8)
    near(0, 0, 2)
    arrived(0, "z4", "z1")
    far(0, 4, 7)
    arrived(0, "sup")
    far(0, 7, 8)
    local[1].wait()
    local[2].wait()
    mlp(0, 4)
    begin(1, "z6", "down", "pairA", "z4")
    far(0, 2, 4)
    arrived(0, "sdown")
    far(0, 0, 2)
    mlp(0, 0)
    begin(1, "z0", "up", "pairB", "z1")

    arrived(1, "z6")
    begin(1, "sdown")
    arrived(1, "pairA", "pairB")
    near(1, 2, 4)
    arrived(1, "down")
    begin(1, "fdown")
    arrived(1, "z0")
    begin(1, "sup")
    near(1, 4, 7)
    arrived(1, "up")
    begin(1, "fup")
    arrived(1, "fdown")
    near(1, 0, 2)
    arrived(1, "fup")
    near(1, 7, 8)
    arrived(1, "z4", "z1")
    far(1, 4, 7)
    arrived(1, "sup")
    far(1, 7, 8)
    local[3].wait()
    local[4].wait()
    mlp(1, 4)
    far(1, 2, 4)
    arrived(1, "sdown")
    far(1, 0, 2)
    mlp(1, 0)

    for layer in range(2):
        for name in NAMES:
            act_on(layer, name, "sent")


def shards(n_polar, n_azimuth, grid, taps, start, count, mix, w_in, w_out):
    copies = 2 * len(NAMES)
    vmem = pl.BlockSpec(memory_space=pltpu.VMEM)
    smem = pl.BlockSpec(memory_space=pltpu.SMEM)
    hbm = pl.BlockSpec(memory_space=pl.ANY)
    return pl.pallas_call(
        functools.partial(body, n_polar, n_azimuth),
        out_shape=jax.ShapeDtypeStruct(grid.shape, grid.dtype),
        in_specs=[hbm, vmem, smem, smem, vmem, hbm, hbm],
        out_specs=vmem,
        scratch_shapes=[
            pltpu.VMEM((2, 11, 128, 640), BF16),
            pltpu.VMEM((2, 11, 64, 640), BF16),
            pltpu.VMEM((8, 576, 512), BF16),
            pltpu.VMEM((8, 576, 256), BF16),
            pltpu.VMEM((2, 640, 1280), BF16),
            pltpu.VMEM((2, 1280, 640), BF16),
            pltpu.VMEM((72, 8, 128), F32),
            pltpu.VMEM((64, 128), F32),
            pltpu.VMEM((64, 128), F32),
            pltpu.VMEM((512, 640), F32),
            pltpu.VMEM((512, 640), BF16),
            pltpu.VMEM((2, 16, 640), F32),
            pltpu.SemaphoreType.DMA((copies,)),
            pltpu.SemaphoreType.DMA((copies,)),
            pltpu.SemaphoreType.DMA((5,)),
        ],
        compiler_params=pltpu.CompilerParams(
            collective_id=0, has_side_effects=True, vmem_limit_bytes=48 * 2**20
        ),
    )(grid, taps, start, count, mix, w_in, w_out)


def solution(mesh):
    return jax.shard_map(
        functools.partial(shards, mesh.shape["polar"], mesh.shape["azimuth"]),
        mesh=mesh,
        in_specs=(
            P("polar", "azimuth", None),
            P("polar", None, None, None),
            P("polar"),
            P("polar"),
            P(),
            P(),
            P(),
        ),
        out_specs=P("polar", "azimuth", None),
        check_vma=False,
    )
```

```python
import functools

import jax
import jax.numpy as jnp
from jax import lax
from jax.experimental import pallas as pl
from jax.experimental.pallas import tpu as pltpu
from jax.sharding import PartitionSpec as P

F32 = jnp.float32
BF16 = jnp.bfloat16
MESH = pl.DeviceIdType.MESH
NAMES = (
    "z0", "z2", "z4", "z6", "p0", "p2", "p4", "p6",
    "down", "up", "sdown", "sup", "fdown", "fup",
)


def gelu(x):
    return 0.5 * x * (1.0 + lax.erf(x * 0.7071067811865476))


def body(
    n_polar, n_azimuth,
    grid, taps_in, start_in, count_in, mix_in, w_in, w_out, out,
    f, band, w1, w2, taps, start, count, mix, src, act, mixf,
    send_sem, recv_sem, local_sem,
):
    p = lax.axis_index("polar")
    a = lax.axis_index("azimuth")
    h = lax.rem(a, 2)
    pair = a + 1 - 2 * h
    zside = lax.rem(a + n_azimuth - 1 + 2 * h, n_azimuth)
    has_low = p > 0
    has_high = p < n_polar - 1
    own = pl.ds(64, 64)
    core_side = pl.ds(pl.multiple_of(128 * (1 - h), 128), 64)
    chip_side = pl.ds(pl.multiple_of(128 * h, 128), 64)

    barrier = pltpu.get_barrier_semaphore()
    for peer in (pair, zside):
        pl.semaphore_signal(barrier, inc=1, device_id=(p, peer), device_id_type=MESH)

    @pl.when(has_low)
    def _():
        pl.semaphore_signal(barrier, inc=1, device_id=(p - 1, a), device_id_type=MESH)

    @pl.when(has_high)
    def _():
        pl.semaphore_signal(barrier, inc=1, device_id=(p + 1, a), device_id_type=MESH)

    def field_rows(layer, row, rows):
        if layer == 0:
            return grid.at[pl.ds(row, rows)]
        return f.at[layer, pl.ds(row + 2, rows), own]

    def transfer(layer, name):
        if name[0] == "z":
            row = int(name[1])
            return (field_rows(layer, row, 2), f.at[layer, pl.ds(row + 2, 2), core_side], (p, zside), None, None)
        if name[0] == "p":
            row = int(name[1])
            return (field_rows(layer, row, 2), f.at[layer, pl.ds(row + 2, 2), chip_side], (p, pair), None, None)
        if name == "down":
            return (field_rows(layer, 6, 2), f.at[layer, pl.ds(0, 2), own], (p + 1, a), has_high, has_low)
        if name == "up":
            return (field_rows(layer, 0, 1), f.at[layer, pl.ds(10, 1), own], (p - 1, a), has_low, has_high)
        if name == "sdown":
            return (f.at[layer, pl.ds(8, 2), chip_side], f.at[layer, pl.ds(0, 2), chip_side], (p + 1, a), has_high, has_low)
        if name == "sup":
            return (f.at[layer, pl.ds(2, 1), chip_side], f.at[layer, pl.ds(10, 1), chip_side], (p - 1, a), has_low, has_high)
        if name == "fdown":
            return (f.at[layer, pl.ds(0, 2), own], f.at[layer, pl.ds(0, 2), chip_side], (p, pair), has_low, has_low)
        return (f.at[layer, pl.ds(10, 1), own], f.at[layer, pl.ds(10, 1), chip_side], (p, pair), has_high, has_high)

    def act_on(layer, name, what):
        source, target, device, sends, receives = transfer(layer, name)
        number = layer * len(NAMES) + NAMES.index(name)
        copy = pltpu.make_async_remote_copy(
            src_ref=source, dst_ref=target, send_sem=send_sem.at[number],
            recv_sem=recv_sem.at[number], device_id=device, device_id_type=MESH,
        )
        run = {"start": copy.start, "recv": copy.wait_recv, "sent": copy.wait_send}[what]
        when = receives if what == "recv" else sends
        if when is None:
            run()
        else:
            pl.when(when)(run)

    def begin(layer, *names):
        for name in names:
            act_on(layer, name, "start")

    def arrived(layer, *names):
        for name in names:
            act_on(layer, name, "recv")

    local = {
        name: pltpu.make_async_copy(source, target, local_sem.at[number])
        for number, (name, source, target) in enumerate((
            ("taps", taps_in, taps),
            ("start", start_in, start),
            ("count", count_in, count),
            ("mix", mix_in, mix),
            ("field", grid, f.at[0, pl.ds(2, 8), own]),
            ("in0", w_in.at[0], w1.at[0]),
            ("out0", w_out.at[0], w2.at[0]),
            ("in1", w_in.at[1], w1.at[1]),
            ("out1", w_out.at[1], w2.at[1]),
        ))
    }
    for copy in local.values():
        copy.start()

    pl.semaphore_wait(barrier, 2 + has_low.astype(jnp.int32) + has_high.astype(jnp.int32))

    begin(0, "z0", "down", "up", "p0", "z2", "p2", "z4", "p4", "z6", "p6")

    @pl.when(p == 0)
    def _():
        for layer in range(2):
            f[layer, 0:2] = jnp.zeros((2, 192, 640), BF16)

    @pl.when(p == n_polar - 1)
    def _():
        for layer in range(2):
            f[layer, 10:11] = jnp.zeros((1, 192, 640), BF16)

    for name in ("taps", "start", "count", "mix"):
        local[name].wait()
    for layer in range(2):
        for k in range(9):
            mixf[layer, k : k + 1] = mix[k, layer : layer + 1].astype(F32)

    offset = lax.broadcasted_iota(jnp.int32, (4, 129), 1) - 64
    lane4 = lax.broadcasted_iota(jnp.int32, (4, 128), 1)
    row4 = lax.broadcasted_iota(jnp.int32, (4, 128), 0)
    lane32 = lax.broadcasted_iota(jnp.int32, (32, 128), 1)
    row32 = lax.broadcasted_iota(jnp.int32, (32, 128), 0)
    ends = ((lane4 + 127 - 32 * row4) & 127) >= 96

    def sources(i, carry):
        inside = (offset >= start[i]) & (offset < start[i] + count[i])
        for k in range(9):
            v = jnp.where(inside, taps[i, k].astype(F32), 0.0)
            low = v[:, 0:128]
            last = jnp.where(lane4 == 0, jnp.broadcast_to(v[:, 128:129], (4, 128)), low)
            tail = last
            for r in range(1, 4):
                tail = jnp.where(row4 == r, pltpu.roll(last, 32 * r, 1), tail)
            src[i * 9 + k, 0:4] = low
            src[i * 9 + k, 4:5] = jnp.sum(jnp.where(ends, tail, 0.0), axis=0, keepdims=True)
        return carry

    def build(i, carry):
        for k in range(9):
            for r in range(5):
                taps_row = jnp.broadcast_to(src[i * 9 + k, r : r + 1, :], (32, 128))
                skewed = pltpu.roll(taps_row, 0, 1, stride=1, stride_axis=0)
                keep = lane32 >= row32 if r < 4 else (lane32 & 31) <= row32
                band[i, 32 * k : 32 * k + 32, 128 * r : 128 * r + 128] = jnp.where(keep, skewed, 0.0).astype(BF16)
        return carry

    lax.fori_loop(0, 8, sources, 0)
    lax.fori_loop(0, 8, build, 0)

    def window(layer, i, half, c0, cw):
        x = 32 * half
        low = f[layer, pl.ds(i, 4), x : x + 128, c0 : c0 + cw].reshape(512, cw)
        high = f[layer, pl.ds(i, 4), x + 128 : x + 160, c0 : c0 + cw].reshape(128, cw)
        return jnp.concatenate([low, high], axis=0)

    def mixed(layer, r, columns):
        def row(k):
            return jnp.concatenate([mixf[layer, k : k + 1, lo:hi] for lo, hi in columns], axis=1)

        total = r[0:32] * row(0)
        for k in range(1, 9):
            total += r[32 * k : 32 * k + 32] * row(k)
        return gelu(total).astype(BF16)

    def conv(layer, lo, hi):
        def one(i, carry):
            for half in range(2):
                rows = pl.ds(pl.multiple_of(i * 64 + 32 * half, 32), 32)
                for c0 in (0, 256):
                    r = jnp.dot(band[i], window(layer, i, half, c0, 256), preferred_element_type=F32)
                    act[rows, c0 : c0 + 256] = mixed(layer, r, ((c0, c0 + 256),))
            both = jnp.concatenate([window(layer, i, half, 512, 128) for half in range(2)], axis=1)
            r = jnp.dot(band[i], both, preferred_element_type=F32)
            m = mixed(layer, r, ((512, 640), (512, 640)))
            for half in range(2):
                rows = pl.ds(pl.multiple_of(i * 64 + 32 * half, 32), 32)
                act[rows, 512:640] = m[:, 128 * half : 128 * half + 128]
            return carry

        lax.fori_loop(lo, hi, one, 0)

    def mlp(layer, row, rows):
        hidden = jnp.dot(act[row * 64 : (row + rows) * 64], w1[layer], preferred_element_type=F32)
        hidden = gelu(hidden).astype(BF16)
        update = jnp.dot(hidden, w2[layer], preferred_element_type=F32)
        field = f[layer, row + 2 : row + 2 + rows, own, :].astype(F32)
        result = (field + update.reshape(rows, 64, 640)).astype(BF16)
        if layer == 0:
            f[1, row + 2 : row + 2 + rows, own, :] = result
        else:
            out[row : row + rows] = result

    local["field"].wait()
    arrived(0, "z0")
    begin(0, "sup")
    arrived(0, "p0", "p2", "z2")
    conv(0, 2, 3)
    arrived(0, "p4", "z4")
    conv(0, 3, 4)
    local["in0"].wait()
    local["out0"].wait()
    mlp(0, 2, 2)
    begin(1, "z2", "p2")
    arrived(0, "down", "up")
    begin(0, "fdown", "fup")
    conv(0, 4, 5)
    arrived(0, "p6", "z6")
    begin(0, "sdown")
    conv(0, 5, 6)
    mlp(0, 4, 2)
    begin(1, "z4", "p4")
    arrived(0, "sup", "fup")
    conv(0, 6, 8)
    mlp(0, 6, 2)
    begin(1, "z6", "down", "p6")
    arrived(0, "sdown", "fdown")
    conv(0, 0, 2)
    mlp(0, 0, 2)
    begin(1, "z0", "up", "p0")

    arrived(1, "z6")
    begin(1, "sdown")
    arrived(1, "p2", "p4", "p6", "z2", "z4")
    conv(1, 4, 5)
    arrived(1, "down")
    begin(1, "fdown")
    conv(1, 5, 7)
    arrived(1, "z0")
    begin(1, "sup")
    arrived(1, "p0")
    conv(1, 2, 4)
    arrived(1, "up")
    begin(1, "fup")
    arrived(1, "sdown", "fdown")
    conv(1, 0, 2)
    local["in1"].wait()
    local["out1"].wait()
    mlp(1, 0, 4)
    arrived(1, "sup", "fup")
    conv(1, 7, 8)
    mlp(1, 4, 4)

    for layer in range(2):
        for name in NAMES:
            act_on(layer, name, "sent")


def shards(n_polar, n_azimuth, grid, taps, start, count, mix, w_in, w_out):
    copies = 2 * len(NAMES)
    hbm = pl.BlockSpec(memory_space=pl.ANY)
    return pl.pallas_call(
        functools.partial(body, n_polar, n_azimuth),
        out_shape=jax.ShapeDtypeStruct(grid.shape, grid.dtype),
        in_specs=[hbm] * 7,
        out_specs=pl.BlockSpec(memory_space=pltpu.VMEM),
        scratch_shapes=[
            pltpu.VMEM((2, 11, 192, 640), BF16),
            pltpu.VMEM((8, 288, 640), BF16),
            pltpu.VMEM(w_in.shape, BF16),
            pltpu.VMEM(w_out.shape, BF16),
            pltpu.VMEM(taps.shape, BF16),
            pltpu.SMEM(start.shape, jnp.int32),
            pltpu.SMEM(count.shape, jnp.int32),
            pltpu.VMEM((9, 2, 640), BF16),
            pltpu.VMEM((72, 8, 128), F32),
            pltpu.VMEM((512, 640), BF16),
            pltpu.VMEM((2, 16, 640), F32),
            pltpu.SemaphoreType.DMA((copies,)),
            pltpu.SemaphoreType.DMA((copies,)),
            pltpu.SemaphoreType.DMA((9,)),
        ],
        compiler_params=pltpu.CompilerParams(
            collective_id=0, has_side_effects=True, vmem_limit_bytes=60 * 2**20
        ),
    )(grid, taps, start, count, jnp.transpose(mix, (1, 0, 2)), w_in, w_out)


def solution(mesh):
    return jax.shard_map(
        functools.partial(shards, mesh.shape["polar"], mesh.shape["azimuth"]),
        mesh=mesh,
        in_specs=(
            P("polar", "azimuth", None),
            P("polar", None, None, None),
            P("polar"),
            P("polar"),
            P(),
            P(),
            P(),
        ),
        out_specs=P("polar", "azimuth", None),
        check_vma=False,
    )
```

```python
import functools

import jax
import jax.numpy as jnp
from jax import lax
from jax.experimental import pallas as pl
from jax.experimental.pallas import tpu as pltpu
from jax.sharding import PartitionSpec as P

F32 = jnp.float32
BF16 = jnp.bfloat16
MESH = pl.DeviceIdType.MESH
NAMES = (
    "z0", "z1", "z2", "z4", "z6", "p0", "p2", "p4", "p6",
    "down", "up", "sdown", "sup", "fdown", "fup",
)


def gelu(x):
    return 0.5 * x * (1.0 + lax.erf(x * 0.7071067811865476))


def body(
    n_polar, n_azimuth,
    grid, taps_in, start_in, count_in, mix_in, w_in, w_out, out,
    f, band, w1, w2, taps, start, count, mix, src, act, mixf, res, part,
    send_sem, recv_sem, local_sem, store_sem,
):
    p = lax.axis_index("polar")
    a = lax.axis_index("azimuth")
    h = lax.rem(a, 2)
    pair = a + 1 - 2 * h
    zside = lax.rem(a + n_azimuth - 1 + 2 * h, n_azimuth)
    has_low = p > 0
    has_high = p < n_polar - 1
    own = pl.ds(64, 64)
    core_side = pl.ds(pl.multiple_of(128 * (1 - h), 128), 64)
    chip_side = pl.ds(pl.multiple_of(128 * h, 128), 64)

    barrier = pltpu.get_barrier_semaphore()
    for peer in (pair, zside):
        pl.semaphore_signal(barrier, inc=1, device_id=(p, peer), device_id_type=MESH)

    @pl.when(has_low)
    def _():
        pl.semaphore_signal(barrier, inc=1, device_id=(p - 1, a), device_id_type=MESH)

    @pl.when(has_high)
    def _():
        pl.semaphore_signal(barrier, inc=1, device_id=(p + 1, a), device_id_type=MESH)

    def field_rows(layer, row, rows):
        return f.at[layer, pl.ds(row + 2, rows), own]

    def transfer(layer, name):
        if name[0] == "z":
            row = int(name[1])
            rows = 1 if row < 2 else 2
            return (field_rows(layer, row, rows), f.at[layer, pl.ds(row + 2, rows), core_side], (p, zside), None, None)
        if name[0] == "p":
            row = int(name[1])
            return (field_rows(layer, row, 2), f.at[layer, pl.ds(row + 2, 2), chip_side], (p, pair), None, None)
        if name == "down":
            return (field_rows(layer, 6, 2), f.at[layer, pl.ds(0, 2), own], (p + 1, a), has_high, has_low)
        if name == "up":
            return (field_rows(layer, 0, 1), f.at[layer, pl.ds(10, 1), own], (p - 1, a), has_low, has_high)
        if name == "sdown":
            return (f.at[layer, pl.ds(8, 2), chip_side], f.at[layer, pl.ds(0, 2), chip_side], (p + 1, a), has_high, has_low)
        if name == "sup":
            return (f.at[layer, pl.ds(2, 1), chip_side], f.at[layer, pl.ds(10, 1), chip_side], (p - 1, a), has_low, has_high)
        if name == "fdown":
            return (f.at[layer, pl.ds(0, 2), own], f.at[layer, pl.ds(0, 2), chip_side], (p, pair), has_low, has_low)
        return (f.at[layer, pl.ds(10, 1), own], f.at[layer, pl.ds(10, 1), chip_side], (p, pair), has_high, has_high)

    def act_on(layer, name, what):
        source, target, device, sends, receives = transfer(layer, name)
        number = layer * len(NAMES) + NAMES.index(name)
        copy = pltpu.make_async_remote_copy(
            src_ref=source, dst_ref=target, send_sem=send_sem.at[number],
            recv_sem=recv_sem.at[number], device_id=device, device_id_type=MESH,
        )
        run = {"start": copy.start, "recv": copy.wait_recv, "sent": copy.wait_send}[what]
        when = receives if what == "recv" else sends
        if when is None:
            run()
        else:
            pl.when(when)(run)

    def begin(layer, *names):
        for name in names:
            act_on(layer, name, "start")

    def arrived(layer, *names):
        for name in names:
            act_on(layer, name, "recv")

    local = {
        name: pltpu.make_async_copy(source, target, local_sem.at[number])
        for number, (name, source, target) in enumerate((
            ("taps", taps_in, taps),
            ("start", start_in, start),
            ("count", count_in, count),
            ("mix", mix_in, mix),
            ("field", grid, f.at[0, pl.ds(2, 8), own]),
            ("in0", w_in.at[0], w1.at[0]),
            ("out0", w_out.at[0], w2.at[0]),
            ("in1", w_in.at[1], w1.at[1]),
            ("out1", w_out.at[1], w2.at[1]),
        ))
    }
    for name in ("field", "taps", "start", "count", "mix"):
        local[name].start()
    local["field"].wait()

    pl.semaphore_wait(barrier, 2 + has_low.astype(jnp.int32) + has_high.astype(jnp.int32))

    begin(0, "z0", "up", "z6", "down", "z4", "p6", "p4", "z2", "p2", "p0", "z1")
    local["in0"].start()
    local["out0"].start()

    @pl.when(p == 0)
    def _():
        for layer in range(2):
            f[layer, 0:2] = jnp.zeros((2, 192, 640), BF16)

    @pl.when(p == n_polar - 1)
    def _():
        for layer in range(2):
            f[layer, 10:11] = jnp.zeros((1, 192, 640), BF16)

    for name in ("taps", "start", "count", "mix"):
        local[name].wait()
    for layer in range(2):
        for k in range(9):
            mixf[layer, k : k + 1] = mix[k, layer : layer + 1].astype(F32)

    even = h == 0
    offset = lax.broadcasted_iota(jnp.int32, (4, 129), 1) - 64
    lane4 = lax.broadcasted_iota(jnp.int32, (4, 128), 1)
    row4 = lax.broadcasted_iota(jnp.int32, (4, 128), 0)
    odd4 = row4 & 1
    lane = lax.broadcasted_iota(jnp.int32, (32, 128), 1)
    row = lax.broadcasted_iota(jnp.int32, (32, 128), 0)
    ends3 = ((lane4 - 97 * h - 32 * row4) & 127) < 32
    ends2 = ((lane4 - 97 * h - 64 * odd4) & 127) < 64
    keep1 = jnp.where(even, jnp.where(lane >= 96, 0, 64 + row - lane), lane - row)
    keep3 = jnp.where(even, (lane & 31) - row, row - (lane & 31))
    keep2 = jnp.where(even, (lane & 63) - row, 32 + row - (lane & 63))

    def sources(i, carry):
        inside = (offset >= start[i]) & (offset < start[i] + count[i])
        for k in range(9):
            v = jnp.where(inside, taps[i, k].astype(F32), 0.0)
            low = v[:, 0:128]
            last = jnp.where(lane4 == 0, jnp.broadcast_to(v[:, 128:129], (4, 128)), low)
            third = jnp.where(even, low, last)
            second = jnp.where(even, low, pltpu.roll(last, 32, 1))
            rolled = third
            for r in range(1, 4):
                rolled = jnp.where(row4 == r, pltpu.roll(third, 32 * r, 1), rolled)
            pairs = jnp.where(odd4 == 1, pltpu.roll(second, 64, 1), second)
            src[i * 9 + k, 0:4] = jnp.where(even, pltpu.roll(last, 64, 1), low)
            src[i * 9 + k, 4:5] = jnp.sum(jnp.where(ends3, rolled, 0.0), axis=0, keepdims=True)
            src[i * 9 + k, 5:6] = jnp.sum(jnp.where(ends2 & (row4 < 2), pairs, 0.0), axis=0, keepdims=True)
            src[i * 9 + k, 6:7] = jnp.sum(jnp.where(ends2 & (row4 >= 2), pairs, 0.0), axis=0, keepdims=True)
        return carry

    def build(i, carry):
        for k in range(9):
            for r in range(7):
                taps_row = jnp.broadcast_to(src[i * 9 + k, r : r + 1, :], (32, 128))
                skewed = pltpu.roll(taps_row, 0, 1, stride=1, stride_axis=0)
                keep = keep1 if r < 4 else (keep3 if r == 4 else keep2)
                band[i, 32 * k : 32 * k + 32, 128 * r : 128 * r + 128] = jnp.where(keep >= 0, skewed, 0.0).astype(BF16)
        return carry

    lax.fori_loop(0, 8, sources, 0)
    lax.fori_loop(0, 8, build, 0)

    def at(x):
        return pl.multiple_of(x, 32)

    halves = (
        (at(96 * (1 - h)), at(64 + 32 * h), at(32 + 96 * h), at(32 * (1 - h))),
        (at(64 - 32 * h), at(32 + 96 * h), at(160 * h), at(32 * h)),
    )

    def piece(layer, i, x, width, c0, cw):
        return f[layer, i : i + 4, pl.ds(x, width), c0 : c0 + cw]

    def first_two(layer, i, half, c0, cw):
        low = piece(layer, i, halves[half][0], 96, c0, cw)
        high = piece(layer, i, halves[half][1], 32, c0, cw)
        return jnp.concatenate([low, high], axis=1).reshape(512, cw)

    def third(layer, i, half, c0, cw):
        return piece(layer, i, halves[half][2], 32, c0, cw).reshape(128, cw)

    def whole(layer, i, half, c0, cw):
        return jnp.concatenate([first_two(layer, i, half, c0, cw), third(layer, i, half, c0, cw)], axis=0)

    def nearby(layer, i, half, c0, cw):
        if half == 0:
            return first_two(layer, i, half, c0, cw)
        low = piece(layer, i, halves[1][0], 96, c0, cw)
        return jnp.concatenate([low, jnp.zeros((4, 32, cw), BF16)], axis=1).reshape(512, cw)

    def mixed(layer, r, columns):
        def weights(k):
            return jnp.concatenate([mixf[layer, k : k + 1, lo:hi] for lo, hi in columns], axis=1)

        total = r[0:32] * weights(0)
        for k in range(1, 9):
            total += r[32 * k : 32 * k + 32] * weights(k)
        return total

    def put(i, half, c0, cw, total):
        rows = pl.ds(pl.multiple_of(i * 64 + halves[half][3], 32), 32)
        act[rows, c0 : c0 + cw] = gelu(total).astype(BF16)

    def tiles(layer, i, lanes, operand, emit):
        for half in range(2):
            for c0 in (0, 256):
                r = jnp.dot(band[i, :, 0:lanes], operand(layer, i, half, c0, 256), preferred_element_type=F32)
                emit(i, half, c0, 256, mixed(layer, r, ((c0, c0 + 256),)))
        both = jnp.concatenate([operand(layer, i, half, 512, 128) for half in range(2)], axis=1)
        r = jnp.dot(band[i, :, 0:lanes], both, preferred_element_type=F32)
        total = mixed(layer, r, ((512, 640), (512, 640)))
        for half in range(2):
            emit(i, half, 512, 128, total[:, 128 * half : 128 * half + 128])

    def conv(layer, *lats):
        for i in lats:
            tiles(layer, i, 640, whole, put)

    def near(layer, *lats):
        def keep(i, half, c0, cw, total):
            part[i, 32 * half : 32 * half + 32, c0 : c0 + cw] = total

        for i in lats:
            tiles(layer, i, 512, nearby, keep)

    def far(layer, *lats):
        for i in lats:
            for c0, cw in ((0, 256), (256, 256), (512, 128)):
                side = f[layer, i : i + 4, chip_side, c0 : c0 + cw].reshape(256, cw)
                for half, columns, operand in (
                    (0, slice(512, 640), third(layer, i, 0, c0, cw)),
                    (1, slice(640, 896), side),
                ):
                    r = jnp.dot(band[i, :, columns], operand, preferred_element_type=F32)
                    before = part[i, 32 * half : 32 * half + 32, c0 : c0 + cw]
                    put(i, half, c0, cw, before + mixed(layer, r, ((c0, c0 + cw),)))

    def store(row, rows):
        return pltpu.make_async_copy(res.at[pl.ds(row, rows)], out.at[pl.ds(row, rows)], store_sem.at[row // 2])

    def mlp(layer, row, rows):
        hidden = jnp.dot(act[row * 64 : (row + rows) * 64], w1[layer], preferred_element_type=F32)
        hidden = gelu(hidden).astype(BF16)
        update = jnp.dot(hidden, w2[layer], preferred_element_type=F32)
        field = f[layer, row + 2 : row + 2 + rows, own, :].astype(F32)
        result = (field + update.reshape(rows, 64, 640)).astype(BF16)
        if layer == 0:
            f[1, row + 2 : row + 2 + rows, own, :] = result
        else:
            res[row : row + rows] = result
            store(row, rows).start()

    local["in1"].start()
    local["out1"].start()
    arrived(0, "p6", "p4", "p2")
    near(0, 6, 5, 4)
    arrived(0, "z0")
    begin(0, "sup")
    arrived(0, "p0")
    near(0, 3, 2)
    arrived(0, "up")
    begin(0, "fup")
    arrived(0, "z6")
    begin(0, "sdown")
    arrived(0, "down")
    begin(0, "fdown")
    arrived(0, "z4")
    far(0, 6)
    arrived(0, "sup", "fup")
    conv(0, 7)
    local["in0"].wait()
    local["out0"].wait()
    mlp(0, 6, 2)
    begin(1, "z6", "down", "p6")
    arrived(0, "z2")
    far(0, 4, 5)
    mlp(0, 4, 2)
    begin(1, "z4", "p4")
    arrived(0, "z1")
    far(0, 2, 3)
    mlp(0, 2, 2)
    begin(1, "z2", "p2")
    arrived(1, "z6")
    begin(1, "sdown")
    arrived(1, "down")
    begin(1, "fdown")
    arrived(0, "sdown", "fdown")
    conv(0, 0, 1)
    mlp(0, 0, 2)
    begin(1, "z0", "up", "p0", "z1")

    arrived(1, "p4", "p6", "z4")
    conv(1, 6)
    arrived(1, "p2", "z2")
    conv(1, 4, 5)
    local["in1"].wait()
    local["out1"].wait()
    mlp(1, 4, 2)
    arrived(1, "z0")
    begin(1, "sup")
    arrived(1, "up")
    begin(1, "fup")
    arrived(1, "p0", "z1", "sdown", "fdown")
    conv(1, 0, 1, 2, 3)
    mlp(1, 0, 4)
    arrived(1, "sup", "fup")
    conv(1, 7)
    mlp(1, 6, 2)

    for row, rows in ((4, 2), (0, 4), (6, 2)):
        store(row, rows).wait()
    for layer in range(2):
        for name in NAMES:
            act_on(layer, name, "sent")


def shards(n_polar, n_azimuth, grid, taps, start, count, mix, w_in, w_out):
    copies = 2 * len(NAMES)
    hbm = pl.BlockSpec(memory_space=pl.ANY)
    return pl.pallas_call(
        functools.partial(body, n_polar, n_azimuth),
        out_shape=jax.ShapeDtypeStruct(grid.shape, grid.dtype),
        in_specs=[hbm] * 7,
        out_specs=hbm,
        scratch_shapes=[
            pltpu.VMEM((2, 11, 192, 640), BF16),
            pltpu.VMEM((8, 288, 896), BF16),
            pltpu.VMEM(w_in.shape, BF16),
            pltpu.VMEM(w_out.shape, BF16),
            pltpu.VMEM(taps.shape, BF16),
            pltpu.SMEM(start.shape, jnp.int32),
            pltpu.SMEM(count.shape, jnp.int32),
            pltpu.VMEM((9, 2, 640), BF16),
            pltpu.VMEM((72, 8, 128), F32),
            pltpu.VMEM((512, 640), BF16),
            pltpu.VMEM((2, 16, 640), F32),
            pltpu.VMEM(grid.shape, BF16),
            pltpu.VMEM(grid.shape, F32),
            pltpu.SemaphoreType.DMA((copies,)),
            pltpu.SemaphoreType.DMA((copies,)),
            pltpu.SemaphoreType.DMA((9,)),
            pltpu.SemaphoreType.DMA((4,)),
        ],
        compiler_params=pltpu.CompilerParams(
            collective_id=0, has_side_effects=True, vmem_limit_bytes=60 * 2**20
        ),
    )(grid, taps, start, count, jnp.transpose(mix, (1, 0, 2)), w_in, w_out)


def solution(mesh):
    return jax.shard_map(
        functools.partial(shards, mesh.shape["polar"], mesh.shape["azimuth"]),
        mesh=mesh,
        in_specs=(
            P("polar", "azimuth", None),
            P("polar", None, None, None),
            P("polar"),
            P("polar"),
            P(),
            P(),
            P(),
        ),
        out_specs=P("polar", "azimuth", None),
        check_vma=False,
    )
```

```python
import functools

import jax
import jax.numpy as jnp
from jax import lax
from jax.experimental import pallas as pl
from jax.experimental.pallas import tpu as pltpu
from jax.sharding import PartitionSpec as P

F32 = jnp.float32
BF16 = jnp.bfloat16
MESH = pl.DeviceIdType.MESH
NAMES = (
    "z0", "z1", "z2", "z4", "z6", "p0", "p2", "p4", "p6",
    "down", "up", "sdown", "sup", "fdown", "fup",
)


def gelu(x):
    return 0.5 * x * (1.0 + lax.erf(x * 0.7071067811865476))


def body(
    n_polar, n_azimuth,
    grid, taps_in, start_in, count_in, mix_in, w_in, w_out, out,
    f, band, w1, w2, taps, start, count, mix, src, act, mixf, res, part,
    send_sem, recv_sem, local_sem, store_sem,
):
    p = lax.axis_index("polar")
    a = lax.axis_index("azimuth")
    h = lax.rem(a, 2)
    pair = a + 1 - 2 * h
    zside = lax.rem(a + n_azimuth - 1 + 2 * h, n_azimuth)
    has_low = p > 0
    has_high = p < n_polar - 1
    own = pl.ds(64, 64)
    core_side = pl.ds(pl.multiple_of(128 * (1 - h), 128), 64)
    chip_side = pl.ds(pl.multiple_of(128 * h, 128), 64)

    barrier = pltpu.get_barrier_semaphore()
    for peer in (pair, zside):
        pl.semaphore_signal(barrier, inc=1, device_id=(p, peer), device_id_type=MESH)

    @pl.when(has_low)
    def _():
        pl.semaphore_signal(barrier, inc=1, device_id=(p - 1, a), device_id_type=MESH)

    @pl.when(has_high)
    def _():
        pl.semaphore_signal(barrier, inc=1, device_id=(p + 1, a), device_id_type=MESH)

    def field_rows(layer, row, rows):
        return f.at[layer, pl.ds(row + 2, rows), own]

    def transfer(layer, name):
        if name[0] == "z":
            row = int(name[1])
            rows = 1 if row < 2 else 2
            return (field_rows(layer, row, rows), f.at[layer, pl.ds(row + 2, rows), core_side], (p, zside), None, None)
        if name[0] == "p":
            row = int(name[1])
            return (field_rows(layer, row, 2), f.at[layer, pl.ds(row + 2, 2), chip_side], (p, pair), None, None)
        if name == "down":
            return (field_rows(layer, 6, 2), f.at[layer, pl.ds(0, 2), own], (p + 1, a), has_high, has_low)
        if name == "up":
            return (field_rows(layer, 0, 1), f.at[layer, pl.ds(10, 1), own], (p - 1, a), has_low, has_high)
        if name == "sdown":
            return (f.at[layer, pl.ds(8, 2), chip_side], f.at[layer, pl.ds(0, 2), chip_side], (p + 1, a), has_high, has_low)
        if name == "sup":
            return (f.at[layer, pl.ds(2, 1), chip_side], f.at[layer, pl.ds(10, 1), chip_side], (p - 1, a), has_low, has_high)
        if name == "fdown":
            return (f.at[layer, pl.ds(0, 2), own], f.at[layer, pl.ds(0, 2), chip_side], (p, pair), has_low, has_low)
        return (f.at[layer, pl.ds(10, 1), own], f.at[layer, pl.ds(10, 1), chip_side], (p, pair), has_high, has_high)

    def act_on(layer, name, what):
        source, target, device, sends, receives = transfer(layer, name)
        number = layer * len(NAMES) + NAMES.index(name)
        copy = pltpu.make_async_remote_copy(
            src_ref=source, dst_ref=target, send_sem=send_sem.at[number],
            recv_sem=recv_sem.at[number], device_id=device, device_id_type=MESH,
        )
        run = {"start": copy.start, "recv": copy.wait_recv, "sent": copy.wait_send}[what]
        when = receives if what == "recv" else sends
        if when is None:
            run()
        else:
            pl.when(when)(run)

    def begin(layer, *names):
        for name in names:
            act_on(layer, name, "start")

    def arrived(layer, *names):
        for name in names:
            act_on(layer, name, "recv")

    local = {
        name: pltpu.make_async_copy(source, target, local_sem.at[number])
        for number, (name, source, target) in enumerate((
            ("taps", taps_in, taps),
            ("start", start_in, start),
            ("count", count_in, count),
            ("mix", mix_in, mix),
            ("field", grid, f.at[0, pl.ds(2, 8), own]),
            ("in0", w_in.at[0], w1.at[0]),
            ("out0", w_out.at[0], w2.at[0]),
            ("in1", w_in.at[1], w1.at[1]),
            ("out1", w_out.at[1], w2.at[1]),
        ))
    }
    for name in ("field", "taps", "start", "count", "mix"):
        local[name].start()
    local["field"].wait()

    pl.semaphore_wait(barrier, 2 + has_low.astype(jnp.int32) + has_high.astype(jnp.int32))

    begin(0, "z0", "up", "z6", "down", "z4", "p6", "p4", "z2", "p2", "p0", "z1")
    local["in0"].start()
    local["out0"].start()

    @pl.when(p == 0)
    def _():
        for layer in range(2):
            f[layer, 0:2] = jnp.zeros((2, 192, 640), BF16)

    @pl.when(p == n_polar - 1)
    def _():
        for layer in range(2):
            f[layer, 10:11] = jnp.zeros((1, 192, 640), BF16)

    for name in ("taps", "start", "count", "mix"):
        local[name].wait()
    for layer in range(2):
        for k in range(9):
            mixf[layer, k : k + 1] = mix[k, layer : layer + 1].astype(F32)

    even = h == 0
    offset = lax.broadcasted_iota(jnp.int32, (4, 129), 1) - 64
    lane4 = lax.broadcasted_iota(jnp.int32, (4, 128), 1)
    row4 = lax.broadcasted_iota(jnp.int32, (4, 128), 0)
    odd4 = row4 & 1
    lane = lax.broadcasted_iota(jnp.int32, (32, 128), 1)
    row = lax.broadcasted_iota(jnp.int32, (32, 128), 0)
    ends3 = ((lane4 - 97 * h - 32 * row4) & 127) < 32
    ends2 = ((lane4 - 97 * h - 64 * odd4) & 127) < 64
    keep1 = jnp.where(even, jnp.where(lane >= 96, 0, 64 + row - lane), lane - row)
    keep3 = jnp.where(even, (lane & 31) - row, row - (lane & 31))
    keep2 = jnp.where(even, (lane & 63) - row, 32 + row - (lane & 63))

    def sources(i, carry):
        inside = (offset >= start[i]) & (offset < start[i] + count[i])
        for k in range(9):
            v = jnp.where(inside, taps[i, k].astype(F32), 0.0)
            low = v[:, 0:128]
            last = jnp.where(lane4 == 0, jnp.broadcast_to(v[:, 128:129], (4, 128)), low)
            third = jnp.where(even, low, last)
            second = jnp.where(even, low, pltpu.roll(last, 32, 1))
            rolled = third
            for r in range(1, 4):
                rolled = jnp.where(row4 == r, pltpu.roll(third, 32 * r, 1), rolled)
            pairs = jnp.where(odd4 == 1, pltpu.roll(second, 64, 1), second)
            src[i * 9 + k, 0:4] = jnp.where(even, pltpu.roll(last, 64, 1), low)
            src[i * 9 + k, 4:5] = jnp.sum(jnp.where(ends3, rolled, 0.0), axis=0, keepdims=True)
            src[i * 9 + k, 5:6] = jnp.sum(jnp.where(ends2 & (row4 < 2), pairs, 0.0), axis=0, keepdims=True)
            src[i * 9 + k, 6:7] = jnp.sum(jnp.where(ends2 & (row4 >= 2), pairs, 0.0), axis=0, keepdims=True)
        return carry

    def build(i, carry):
        for k in range(9):
            for r in range(7):
                taps_row = jnp.broadcast_to(src[i * 9 + k, r : r + 1, :], (32, 128))
                skewed = pltpu.roll(taps_row, 0, 1, stride=1, stride_axis=0)
                keep = keep1 if r < 4 else (keep3 if r == 4 else keep2)
                band[i, 32 * k : 32 * k + 32, 128 * r : 128 * r + 128] = jnp.where(keep >= 0, skewed, 0.0).astype(BF16)
        return carry

    lax.fori_loop(0, 8, sources, 0)
    lax.fori_loop(0, 8, build, 0)

    def at(x):
        return pl.multiple_of(x, 32)

    halves = (
        (at(96 * (1 - h)), at(64 + 32 * h), at(32 + 96 * h), at(32 * (1 - h))),
        (at(64 - 32 * h), at(32 + 96 * h), at(160 * h), at(32 * h)),
    )

    def piece(layer, i, x, width, c0, cw):
        return f[layer, i : i + 4, pl.ds(x, width), c0 : c0 + cw]

    def first_two(layer, i, half, c0, cw):
        low = piece(layer, i, halves[half][0], 96, c0, cw)
        high = piece(layer, i, halves[half][1], 32, c0, cw)
        return jnp.concatenate([low, high], axis=1).reshape(512, cw)

    def third(layer, i, half, c0, cw):
        return piece(layer, i, halves[half][2], 32, c0, cw).reshape(128, cw)

    def whole(layer, i, half, c0, cw):
        return jnp.concatenate([first_two(layer, i, half, c0, cw), third(layer, i, half, c0, cw)], axis=0)

    def nearby(layer, i, half, c0, cw):
        if half == 0:
            return first_two(layer, i, half, c0, cw)
        low = piece(layer, i, halves[1][0], 96, c0, cw)
        return jnp.concatenate([low, jnp.zeros((4, 32, cw), BF16)], axis=1).reshape(512, cw)

    def mixed(layer, r, columns):
        def weights(k):
            return jnp.concatenate([mixf[layer, k : k + 1, lo:hi] for lo, hi in columns], axis=1)

        total = r[0:32] * weights(0)
        for k in range(1, 9):
            total += r[32 * k : 32 * k + 32] * weights(k)
        return total

    def put(i, half, c0, cw, total):
        rows = pl.ds(pl.multiple_of(i * 64 + halves[half][3], 32), 32)
        act[rows, c0 : c0 + cw] = gelu(total).astype(BF16)

    def tiles(layer, i, lanes, operand, emit):
        for half in range(2):
            for c0 in (0, 256):
                r = jnp.dot(band[i, :, 0:lanes], operand(layer, i, half, c0, 256), preferred_element_type=F32)
                emit(i, half, c0, 256, mixed(layer, r, ((c0, c0 + 256),)))
        both = jnp.concatenate([operand(layer, i, half, 512, 128) for half in range(2)], axis=1)
        r = jnp.dot(band[i, :, 0:lanes], both, preferred_element_type=F32)
        total = mixed(layer, r, ((512, 640), (512, 640)))
        for half in range(2):
            emit(i, half, 512, 128, total[:, 128 * half : 128 * half + 128])

    def conv(layer, *lats):
        for i in lats:
            tiles(layer, i, 640, whole, put)

    def near(layer, *lats):
        def keep(i, half, c0, cw, total):
            part[i, 32 * half : 32 * half + 32, c0 : c0 + cw] = total

        for i in lats:
            tiles(layer, i, 512, nearby, keep)

    def far(layer, *lats):
        for i in lats:
            for c0, cw in ((0, 256), (256, 256), (512, 128)):
                side = f[layer, i : i + 4, chip_side, c0 : c0 + cw].reshape(256, cw)
                for half, columns, operand in (
                    (0, slice(512, 640), third(layer, i, 0, c0, cw)),
                    (1, slice(640, 896), side),
                ):
                    r = jnp.dot(band[i, :, columns], operand, preferred_element_type=F32)
                    before = part[i, 32 * half : 32 * half + 32, c0 : c0 + cw]
                    put(i, half, c0, cw, before + mixed(layer, r, ((c0, c0 + cw),)))

    def store(row, rows):
        return pltpu.make_async_copy(res.at[pl.ds(row, rows)], out.at[pl.ds(row, rows)], store_sem.at[row // 2])

    def mlp(layer, row, rows):
        hidden = jnp.dot(act[row * 64 : (row + rows) * 64], w1[layer], preferred_element_type=F32)
        hidden = gelu(hidden).astype(BF16)
        update = jnp.dot(hidden, w2[layer], preferred_element_type=F32)
        field = f[layer, row + 2 : row + 2 + rows, own, :].astype(F32)
        result = (field + update.reshape(rows, 64, 640)).astype(BF16)
        if layer == 0:
            f[1, row + 2 : row + 2 + rows, own, :] = result
        else:
            res[row : row + rows] = result
            store(row, rows).start()

    local["in1"].start()
    local["out1"].start()
    arrived(0, "p6", "p4", "p2")
    near(0, 6, 5, 4)
    arrived(0, "z0")
    begin(0, "sup")
    arrived(0, "p0")
    near(0, 3, 2)
    arrived(0, "up")
    begin(0, "fup")
    arrived(0, "z6")
    begin(0, "sdown")
    arrived(0, "down")
    begin(0, "fdown")
    arrived(0, "z4")
    far(0, 6)
    arrived(0, "sup", "fup")
    conv(0, 7)
    local["in0"].wait()
    local["out0"].wait()
    mlp(0, 6, 2)
    begin(1, "z6", "down", "p6")
    arrived(0, "z2")
    far(0, 4, 5)
    mlp(0, 4, 2)
    begin(1, "z4", "p4")
    arrived(0, "z1")
    far(0, 2, 3)
    mlp(0, 2, 2)
    begin(1, "z2", "p2")
    arrived(0, "sdown", "fdown")
    conv(0, 0, 1)
    arrived(1, "z6")
    begin(1, "sdown")
    mlp(0, 0, 2)
    begin(1, "z0", "up", "p0", "z1")

    arrived(1, "p4", "p6", "z4")
    conv(1, 6)
    arrived(1, "down")
    begin(1, "fdown")
    arrived(1, "p2", "z2")
    conv(1, 4, 5)
    arrived(1, "z0")
    begin(1, "sup")
    arrived(1, "up")
    begin(1, "fup")
    local["in1"].wait()
    local["out1"].wait()
    mlp(1, 4, 2)
    arrived(1, "p0", "z1")
    conv(1, 2, 3)
    arrived(1, "sdown", "fdown")
    conv(1, 0, 1)
    mlp(1, 0, 4)
    arrived(1, "sup", "fup")
    conv(1, 7)
    mlp(1, 6, 2)

    for row, rows in ((4, 2), (0, 4), (6, 2)):
        store(row, rows).wait()
    for layer in range(2):
        for name in NAMES:
            act_on(layer, name, "sent")


def shards(n_polar, n_azimuth, grid, taps, start, count, mix, w_in, w_out):
    copies = 2 * len(NAMES)
    hbm = pl.BlockSpec(memory_space=pl.ANY)
    return pl.pallas_call(
        functools.partial(body, n_polar, n_azimuth),
        out_shape=jax.ShapeDtypeStruct(grid.shape, grid.dtype),
        in_specs=[hbm] * 7,
        out_specs=hbm,
        scratch_shapes=[
            pltpu.VMEM((2, 11, 192, 640), BF16),
            pltpu.VMEM((8, 288, 896), BF16),
            pltpu.VMEM(w_in.shape, BF16),
            pltpu.VMEM(w_out.shape, BF16),
            pltpu.VMEM(taps.shape, BF16),
            pltpu.SMEM(start.shape, jnp.int32),
            pltpu.SMEM(count.shape, jnp.int32),
            pltpu.VMEM((9, 2, 640), BF16),
            pltpu.VMEM((72, 8, 128), F32),
            pltpu.VMEM((512, 640), BF16),
            pltpu.VMEM((2, 16, 640), F32),
            pltpu.VMEM(grid.shape, BF16),
            pltpu.VMEM(grid.shape, F32),
            pltpu.SemaphoreType.DMA((copies,)),
            pltpu.SemaphoreType.DMA((copies,)),
            pltpu.SemaphoreType.DMA((9,)),
            pltpu.SemaphoreType.DMA((4,)),
        ],
        compiler_params=pltpu.CompilerParams(
            collective_id=0, has_side_effects=True, vmem_limit_bytes=60 * 2**20
        ),
    )(grid, taps, start, count, jnp.transpose(mix, (1, 0, 2)), w_in, w_out)


def solution(mesh):
    return jax.shard_map(
        functools.partial(shards, mesh.shape["polar"], mesh.shape["azimuth"]),
        mesh=mesh,
        in_specs=(
            P("polar", "azimuth", None),
            P("polar", None, None, None),
            P("polar"),
            P("polar"),
            P(),
            P(),
            P(),
        ),
        out_specs=P("polar", "azimuth", None),
        check_vma=False,
    )
```

```python
import functools

import jax
import jax.numpy as jnp
from jax import lax
from jax.experimental import pallas as pl
from jax.experimental.pallas import tpu as pltpu
from jax.sharding import PartitionSpec as P

F32 = jnp.float32
BF16 = jnp.bfloat16
MESH = pl.DeviceIdType.MESH
NAMES = (
    "z0", "z1", "z2", "z4", "z6", "p0", "p2", "p4", "p6",
    "down", "up", "sdown", "sup", "fdown", "fup",
)


def gelu(x):
    return 0.5 * x * (1.0 + lax.erf(x * 0.7071067811865476))


def body(
    n_polar, n_azimuth,
    grid, taps_in, start_in, count_in, mix_in, w_in, w_out, out,
    f, band, w1, w2, taps, start, count, mix, src, act, mixf, res, part,
    send_sem, recv_sem, local_sem, store_sem,
):
    p = lax.axis_index("polar")
    a = lax.axis_index("azimuth")
    h = lax.rem(a, 2)
    pair = a + 1 - 2 * h
    zside = lax.rem(a + n_azimuth - 1 + 2 * h, n_azimuth)
    has_low = p > 0
    has_high = p < n_polar - 1
    own = pl.ds(64, 64)
    core_side = pl.ds(pl.multiple_of(128 * (1 - h), 128), 64)
    chip_side = pl.ds(pl.multiple_of(128 * h, 128), 64)

    barrier = pltpu.get_barrier_semaphore()
    for peer in (pair, zside):
        pl.semaphore_signal(barrier, inc=1, device_id=(p, peer), device_id_type=MESH)

    @pl.when(has_low)
    def _():
        pl.semaphore_signal(barrier, inc=1, device_id=(p - 1, a), device_id_type=MESH)

    @pl.when(has_high)
    def _():
        pl.semaphore_signal(barrier, inc=1, device_id=(p + 1, a), device_id_type=MESH)

    def field_rows(layer, row, rows):
        return f.at[layer, pl.ds(row + 2, rows), own]

    def transfer(layer, name):
        if name[0] == "z":
            row = int(name[1])
            rows = 1 if row < 2 else 2
            return (field_rows(layer, row, rows), f.at[layer, pl.ds(row + 2, rows), core_side], (p, zside), None, None)
        if name[0] == "p":
            row = int(name[1])
            return (field_rows(layer, row, 2), f.at[layer, pl.ds(row + 2, 2), chip_side], (p, pair), None, None)
        if name == "down":
            return (field_rows(layer, 6, 2), f.at[layer, pl.ds(0, 2), own], (p + 1, a), has_high, has_low)
        if name == "up":
            return (field_rows(layer, 0, 1), f.at[layer, pl.ds(10, 1), own], (p - 1, a), has_low, has_high)
        if name == "sdown":
            return (f.at[layer, pl.ds(8, 2), chip_side], f.at[layer, pl.ds(0, 2), chip_side], (p + 1, a), has_high, has_low)
        if name == "sup":
            return (f.at[layer, pl.ds(2, 1), chip_side], f.at[layer, pl.ds(10, 1), chip_side], (p - 1, a), has_low, has_high)
        if name == "fdown":
            return (f.at[layer, pl.ds(0, 2), own], f.at[layer, pl.ds(0, 2), chip_side], (p, pair), has_low, has_low)
        return (f.at[layer, pl.ds(10, 1), own], f.at[layer, pl.ds(10, 1), chip_side], (p, pair), has_high, has_high)

    def act_on(layer, name, what):
        source, target, device, sends, receives = transfer(layer, name)
        number = layer * len(NAMES) + NAMES.index(name)
        copy = pltpu.make_async_remote_copy(
            src_ref=source, dst_ref=target, send_sem=send_sem.at[number],
            recv_sem=recv_sem.at[number], device_id=device, device_id_type=MESH,
        )
        run = {"start": copy.start, "recv": copy.wait_recv, "sent": copy.wait_send}[what]
        when = receives if what == "recv" else sends
        if when is None:
            run()
        else:
            pl.when(when)(run)

    def begin(layer, *names):
        for name in names:
            act_on(layer, name, "start")

    def arrived(layer, *names):
        for name in names:
            act_on(layer, name, "recv")

    local = {
        name: pltpu.make_async_copy(source, target, local_sem.at[number])
        for number, (name, source, target) in enumerate((
            ("taps", taps_in, taps),
            ("start", start_in, start),
            ("count", count_in, count),
            ("mix", mix_in, mix),
            ("field", grid, f.at[0, pl.ds(2, 8), own]),
            ("in0", w_in.at[0], w1.at[0]),
            ("out0", w_out.at[0], w2.at[0]),
            ("in1", w_in.at[1], w1.at[1]),
            ("out1", w_out.at[1], w2.at[1]),
        ))
    }
    for name in ("field", "taps", "start", "count", "mix"):
        local[name].start()
    local["field"].wait()

    pl.semaphore_wait(barrier, 2 + has_low.astype(jnp.int32) + has_high.astype(jnp.int32))

    begin(0, "z0", "up", "z6", "down", "z4", "p6", "p4", "z2", "p2", "p0", "z1")
    local["in0"].start()
    local["out0"].start()

    @pl.when(p == 0)
    def _():
        for layer in range(2):
            f[layer, 0:2] = jnp.zeros((2, 192, 640), BF16)

    @pl.when(p == n_polar - 1)
    def _():
        for layer in range(2):
            f[layer, 10:11] = jnp.zeros((1, 192, 640), BF16)

    for name in ("taps", "start", "count", "mix"):
        local[name].wait()
    for layer in range(2):
        for k in range(9):
            mixf[layer, k : k + 1] = mix[k, layer : layer + 1].astype(F32)

    even = h == 0
    offset = lax.broadcasted_iota(jnp.int32, (4, 129), 1) - 64
    lane4 = lax.broadcasted_iota(jnp.int32, (4, 128), 1)
    row4 = lax.broadcasted_iota(jnp.int32, (4, 128), 0)
    odd4 = row4 & 1
    lane = lax.broadcasted_iota(jnp.int32, (32, 128), 1)
    row = lax.broadcasted_iota(jnp.int32, (32, 128), 0)
    ends3 = ((lane4 - 97 * h - 32 * row4) & 127) < 32
    ends2 = ((lane4 - 97 * h - 64 * odd4) & 127) < 64
    keep1 = jnp.where(even, jnp.where(lane >= 96, 0, 64 + row - lane), lane - row)
    keep3 = jnp.where(even, (lane & 31) - row, row - (lane & 31))
    keep2 = jnp.where(even, (lane & 63) - row, 32 + row - (lane & 63))

    def sources(i, carry):
        inside = (offset >= start[i]) & (offset < start[i] + count[i])
        for k in range(9):
            v = jnp.where(inside, taps[i, k].astype(F32), 0.0)
            low = v[:, 0:128]
            last = jnp.where(lane4 == 0, jnp.broadcast_to(v[:, 128:129], (4, 128)), low)
            third = jnp.where(even, low, last)
            second = jnp.where(even, low, pltpu.roll(last, 32, 1))
            rolled = third
            for r in range(1, 4):
                rolled = jnp.where(row4 == r, pltpu.roll(third, 32 * r, 1), rolled)
            pairs = jnp.where(odd4 == 1, pltpu.roll(second, 64, 1), second)
            src[i * 9 + k, 0:4] = jnp.where(even, pltpu.roll(last, 64, 1), low)
            src[i * 9 + k, 4:5] = jnp.sum(jnp.where(ends3, rolled, 0.0), axis=0, keepdims=True)
            src[i * 9 + k, 5:6] = jnp.sum(jnp.where(ends2 & (row4 < 2), pairs, 0.0), axis=0, keepdims=True)
            src[i * 9 + k, 6:7] = jnp.sum(jnp.where(ends2 & (row4 >= 2), pairs, 0.0), axis=0, keepdims=True)
        return carry

    def build(i, carry):
        for k in range(9):
            for r in range(7):
                taps_row = jnp.broadcast_to(src[i * 9 + k, r : r + 1, :], (32, 128))
                skewed = pltpu.roll(taps_row, 0, 1, stride=1, stride_axis=0)
                keep = keep1 if r < 4 else (keep3 if r == 4 else keep2)
                band[i, 32 * k : 32 * k + 32, 128 * r : 128 * r + 128] = jnp.where(keep >= 0, skewed, 0.0).astype(BF16)
        return carry

    lax.fori_loop(0, 8, sources, 0)
    lax.fori_loop(0, 8, build, 0)

    def at(x):
        return pl.multiple_of(x, 32)

    halves = (
        (at(96 * (1 - h)), at(64 + 32 * h), at(32 + 96 * h), at(32 * (1 - h))),
        (at(64 - 32 * h), at(32 + 96 * h), at(160 * h), at(32 * h)),
    )

    def piece(layer, i, x, width, c0, cw):
        return f[layer, i : i + 4, pl.ds(x, width), c0 : c0 + cw]

    def first_two(layer, i, half, c0, cw):
        low = piece(layer, i, halves[half][0], 96, c0, cw)
        high = piece(layer, i, halves[half][1], 32, c0, cw)
        return jnp.concatenate([low, high], axis=1).reshape(512, cw)

    def third(layer, i, half, c0, cw):
        return piece(layer, i, halves[half][2], 32, c0, cw).reshape(128, cw)

    def whole(layer, i, half, c0, cw):
        return jnp.concatenate([first_two(layer, i, half, c0, cw), third(layer, i, half, c0, cw)], axis=0)

    def nearby(layer, i, half, c0, cw):
        if half == 0:
            return first_two(layer, i, half, c0, cw)
        low = piece(layer, i, halves[1][0], 96, c0, cw)
        return jnp.concatenate([low, jnp.zeros((4, 32, cw), BF16)], axis=1).reshape(512, cw)

    def mixed(layer, r, columns):
        def weights(k):
            return jnp.concatenate([mixf[layer, k : k + 1, lo:hi] for lo, hi in columns], axis=1)

        total = r[0:32] * weights(0)
        for k in range(1, 9):
            total += r[32 * k : 32 * k + 32] * weights(k)
        return total

    def put(i, half, c0, cw, total):
        rows = pl.ds(pl.multiple_of(i * 64 + halves[half][3], 32), 32)
        act[rows, c0 : c0 + cw] = gelu(total).astype(BF16)

    def tiles(layer, i, lanes, operand, emit):
        for half in range(2):
            for c0 in (0, 256):
                r = jnp.dot(band[i, :, 0:lanes], operand(layer, i, half, c0, 256), preferred_element_type=F32)
                emit(i, half, c0, 256, mixed(layer, r, ((c0, c0 + 256),)))
        both = jnp.concatenate([operand(layer, i, half, 512, 128) for half in range(2)], axis=1)
        r = jnp.dot(band[i, :, 0:lanes], both, preferred_element_type=F32)
        total = mixed(layer, r, ((512, 640), (512, 640)))
        for half in range(2):
            emit(i, half, 512, 128, total[:, 128 * half : 128 * half + 128])

    def conv(layer, *lats):
        for i in lats:
            tiles(layer, i, 640, whole, put)

    def near(layer, *lats):
        def keep(i, half, c0, cw, total):
            part[i, 32 * half : 32 * half + 32, c0 : c0 + cw] = total

        for i in lats:
            tiles(layer, i, 512, nearby, keep)

    def far(layer, *lats):
        for i in lats:
            for c0, cw in ((0, 256), (256, 256), (512, 128)):
                side = f[layer, i : i + 4, chip_side, c0 : c0 + cw].reshape(256, cw)
                for half, columns, operand in (
                    (0, slice(512, 640), third(layer, i, 0, c0, cw)),
                    (1, slice(640, 896), side),
                ):
                    r = jnp.dot(band[i, :, columns], operand, preferred_element_type=F32)
                    before = part[i, 32 * half : 32 * half + 32, c0 : c0 + cw]
                    put(i, half, c0, cw, before + mixed(layer, r, ((c0, c0 + cw),)))

    def store(row, rows):
        return pltpu.make_async_copy(res.at[pl.ds(row, rows)], out.at[pl.ds(row, rows)], store_sem.at[row // 2])

    def mlp(layer, row, rows):
        hidden = jnp.dot(act[row * 64 : (row + rows) * 64], w1[layer], preferred_element_type=F32)
        hidden = gelu(hidden).astype(BF16)
        update = jnp.dot(hidden, w2[layer], preferred_element_type=F32)
        field = f[layer, row + 2 : row + 2 + rows, own, :].astype(F32)
        result = (field + update.reshape(rows, 64, 640)).astype(BF16)
        if layer == 0:
            f[1, row + 2 : row + 2 + rows, own, :] = result
        else:
            res[row : row + rows] = result
            store(row, rows).start()

    local["in1"].start()
    local["out1"].start()
    arrived(0, "p6", "p4", "p2")
    near(0, 6, 5, 4)
    arrived(0, "z0")
    begin(0, "sup")
    arrived(0, "p0")
    near(0, 3, 2)
    arrived(0, "up")
    begin(0, "fup")
    arrived(0, "z6")
    begin(0, "sdown")
    arrived(0, "down")
    begin(0, "fdown")
    arrived(0, "z4")
    far(0, 6)
    arrived(0, "sup", "fup")
    conv(0, 7)
    local["in0"].wait()
    local["out0"].wait()
    mlp(0, 6, 2)
    begin(1, "z6", "down", "p6")
    arrived(0, "z2")
    far(0, 4, 5)
    mlp(0, 4, 2)
    begin(1, "z4", "p4")
    arrived(0, "z1")
    far(0, 2, 3)
    mlp(0, 2, 2)
    begin(1, "z2", "p2")
    arrived(0, "sdown", "fdown")
    conv(0, 0, 1)
    arrived(1, "z6")
    begin(1, "sdown")
    mlp(0, 0, 2)
    begin(1, "z0", "up", "p0", "z1")

    arrived(1, "p4", "p6", "z4")
    conv(1, 6)
    arrived(1, "p2")
    near(1, 5, 4)
    arrived(1, "z2")
    far(1, 4, 5)
    arrived(1, "down")
    begin(1, "fdown")
    arrived(1, "z0")
    begin(1, "sup")
    arrived(1, "up")
    begin(1, "fup")
    local["in1"].wait()
    local["out1"].wait()
    mlp(1, 4, 2)
    arrived(1, "p0", "z1")
    conv(1, 2, 3)
    arrived(1, "sdown", "fdown")
    conv(1, 0, 1)
    mlp(1, 0, 4)
    arrived(1, "sup", "fup")
    conv(1, 7)
    mlp(1, 6, 2)

    for row, rows in ((4, 2), (0, 4), (6, 2)):
        store(row, rows).wait()
    for layer in range(2):
        for name in NAMES:
            act_on(layer, name, "sent")


def shards(n_polar, n_azimuth, grid, taps, start, count, mix, w_in, w_out):
    copies = 2 * len(NAMES)
    hbm = pl.BlockSpec(memory_space=pl.ANY)
    return pl.pallas_call(
        functools.partial(body, n_polar, n_azimuth),
        out_shape=jax.ShapeDtypeStruct(grid.shape, grid.dtype),
        in_specs=[hbm] * 7,
        out_specs=hbm,
        scratch_shapes=[
            pltpu.VMEM((2, 11, 192, 640), BF16),
            pltpu.VMEM((8, 288, 896), BF16),
            pltpu.VMEM(w_in.shape, BF16),
            pltpu.VMEM(w_out.shape, BF16),
            pltpu.VMEM(taps.shape, BF16),
            pltpu.SMEM(start.shape, jnp.int32),
            pltpu.SMEM(count.shape, jnp.int32),
            pltpu.VMEM((9, 2, 640), BF16),
            pltpu.VMEM((72, 8, 128), F32),
            pltpu.VMEM((512, 640), BF16),
            pltpu.VMEM((2, 16, 640), F32),
            pltpu.VMEM(grid.shape, BF16),
            pltpu.VMEM(grid.shape, F32),
            pltpu.SemaphoreType.DMA((copies,)),
            pltpu.SemaphoreType.DMA((copies,)),
            pltpu.SemaphoreType.DMA((9,)),
            pltpu.SemaphoreType.DMA((4,)),
        ],
        compiler_params=pltpu.CompilerParams(
            collective_id=0, has_side_effects=True, vmem_limit_bytes=60 * 2**20
        ),
    )(grid, taps, start, count, jnp.transpose(mix, (1, 0, 2)), w_in, w_out)


def solution(mesh):
    return jax.shard_map(
        functools.partial(shards, mesh.shape["polar"], mesh.shape["azimuth"]),
        mesh=mesh,
        in_specs=(
            P("polar", "azimuth", None),
            P("polar", None, None, None),
            P("polar"),
            P("polar"),
            P(),
            P(),
            P(),
        ),
        out_specs=P("polar", "azimuth", None),
        check_vma=False,
    )
```

```python
import functools

import jax
import jax.numpy as jnp
from jax import lax
from jax.experimental import pallas as pl
from jax.experimental.pallas import tpu as pltpu
from jax.sharding import PartitionSpec as P

F32 = jnp.float32
BF16 = jnp.bfloat16
MESH = pl.DeviceIdType.MESH
NAMES = (
    "z0", "z1", "z2", "z4", "z6", "p0", "p2", "p4", "p6",
    "down", "up", "sdown", "sup", "fdown", "fup",
)


def gelu(x):
    return 0.5 * x * (1.0 + lax.erf(x * 0.7071067811865476))


def body(
    n_polar, n_azimuth,
    grid, taps_in, start_in, count_in, mix_in, w_in, w_out, out,
    f, band, w1, w2, taps, start, count, mix, src, act, mixf, res, part,
    send_sem, recv_sem, local_sem, store_sem,
):
    p = lax.axis_index("polar")
    a = lax.axis_index("azimuth")
    h = lax.rem(a, 2)
    pair = a + 1 - 2 * h
    zside = lax.rem(a + n_azimuth - 1 + 2 * h, n_azimuth)
    has_low = p > 0
    has_high = p < n_polar - 1
    own = pl.ds(64, 64)
    core_side = pl.ds(pl.multiple_of(128 * (1 - h), 128), 64)
    chip_side = pl.ds(pl.multiple_of(128 * h, 128), 64)

    barrier = pltpu.get_barrier_semaphore()
    for peer in (pair, zside):
        pl.semaphore_signal(barrier, inc=1, device_id=(p, peer), device_id_type=MESH)

    @pl.when(has_low)
    def _():
        for peer in (a, zside):
            pl.semaphore_signal(barrier, inc=1, device_id=(p - 1, peer), device_id_type=MESH)

    @pl.when(has_high)
    def _():
        for peer in (a, zside):
            pl.semaphore_signal(barrier, inc=1, device_id=(p + 1, peer), device_id_type=MESH)

    def field_rows(layer, row, rows):
        return f.at[layer, pl.ds(row + 2, rows), own]

    def transfer(layer, name):
        if name[0] == "z":
            row = int(name[1])
            rows = 1 if row < 2 else 2
            return (field_rows(layer, row, rows), f.at[layer, pl.ds(row + 2, rows), core_side], (p, zside), None, None)
        if name[0] == "p":
            row = int(name[1])
            return (field_rows(layer, row, 2), f.at[layer, pl.ds(row + 2, 2), chip_side], (p, pair), None, None)
        if name == "down":
            return (field_rows(layer, 6, 2), f.at[layer, pl.ds(0, 2), own], (p + 1, a), has_high, has_low)
        if name == "up":
            return (field_rows(layer, 0, 1), f.at[layer, pl.ds(10, 1), own], (p - 1, a), has_low, has_high)
        if name == "sdown":
            return (f.at[layer, pl.ds(8, 2), chip_side], f.at[layer, pl.ds(0, 2), chip_side], (p + 1, a), has_high, has_low)
        if name == "sup" and layer == 0:
            return (field_rows(0, 0, 1), f.at[0, pl.ds(10, 1), core_side], (p - 1, zside), has_low, has_high)
        if name == "sup":
            return (f.at[layer, pl.ds(2, 1), chip_side], f.at[layer, pl.ds(10, 1), chip_side], (p - 1, a), has_low, has_high)
        if name == "fdown":
            return (f.at[layer, pl.ds(0, 2), own], f.at[layer, pl.ds(0, 2), chip_side], (p, pair), has_low, has_low)
        return (f.at[layer, pl.ds(10, 1), own], f.at[layer, pl.ds(10, 1), chip_side], (p, pair), has_high, has_high)

    def act_on(layer, name, what):
        source, target, device, sends, receives = transfer(layer, name)
        number = layer * len(NAMES) + NAMES.index(name)
        copy = pltpu.make_async_remote_copy(
            src_ref=source, dst_ref=target, send_sem=send_sem.at[number],
            recv_sem=recv_sem.at[number], device_id=device, device_id_type=MESH,
        )
        run = {"start": copy.start, "recv": copy.wait_recv, "sent": copy.wait_send}[what]
        when = receives if what == "recv" else sends
        if when is None:
            run()
        else:
            pl.when(when)(run)

    def begin(layer, *names):
        for name in names:
            act_on(layer, name, "start")

    def arrived(layer, *names):
        for name in names:
            act_on(layer, name, "recv")

    local = {
        name: pltpu.make_async_copy(source, target, local_sem.at[number])
        for number, (name, source, target) in enumerate((
            ("taps", taps_in, taps),
            ("start", start_in, start),
            ("count", count_in, count),
            ("mix", mix_in, mix),
            ("field", grid, f.at[0, pl.ds(2, 8), own]),
            ("in0", w_in.at[0], w1.at[0]),
            ("out0", w_out.at[0], w2.at[0]),
            ("in1", w_in.at[1], w1.at[1]),
            ("out1", w_out.at[1], w2.at[1]),
        ))
    }
    for name in ("field", "taps", "start", "count", "mix"):
        local[name].start()
    local["field"].wait()

    pl.semaphore_wait(barrier, 2 + 2 * has_low.astype(jnp.int32) + 2 * has_high.astype(jnp.int32))

    begin(0, "sup", "up", "z6", "down", "z4", "p6", "p4", "z2", "p2", "p0", "z0", "z1")
    local["in0"].start()
    local["out0"].start()

    @pl.when(p == 0)
    def _():
        for layer in range(2):
            f[layer, 0:2] = jnp.zeros((2, 192, 640), BF16)

    @pl.when(p == n_polar - 1)
    def _():
        for layer in range(2):
            f[layer, 10:11] = jnp.zeros((1, 192, 640), BF16)

    for name in ("taps", "start", "count", "mix"):
        local[name].wait()
    for layer in range(2):
        for k in range(9):
            mixf[layer, k : k + 1] = mix[k, layer : layer + 1].astype(F32)

    even = h == 0
    offset = lax.broadcasted_iota(jnp.int32, (4, 129), 1) - 64
    lane4 = lax.broadcasted_iota(jnp.int32, (4, 128), 1)
    row4 = lax.broadcasted_iota(jnp.int32, (4, 128), 0)
    odd4 = row4 & 1
    lane = lax.broadcasted_iota(jnp.int32, (32, 128), 1)
    row = lax.broadcasted_iota(jnp.int32, (32, 128), 0)
    ends3 = ((lane4 - 97 * h - 32 * row4) & 127) < 32
    ends2 = ((lane4 - 97 * h - 64 * odd4) & 127) < 64
    keep1 = jnp.where(even, jnp.where(lane >= 96, 0, 64 + row - lane), lane - row)
    keep3 = jnp.where(even, (lane & 31) - row, row - (lane & 31))
    keep2 = jnp.where(even, (lane & 63) - row, 32 + row - (lane & 63))

    def sources(i, carry):
        inside = (offset >= start[i]) & (offset < start[i] + count[i])
        for k in range(9):
            v = jnp.where(inside, taps[i, k].astype(F32), 0.0)
            low = v[:, 0:128]
            last = jnp.where(lane4 == 0, jnp.broadcast_to(v[:, 128:129], (4, 128)), low)
            third = jnp.where(even, low, last)
            second = jnp.where(even, low, pltpu.roll(last, 32, 1))
            rolled = third
            for r in range(1, 4):
                rolled = jnp.where(row4 == r, pltpu.roll(third, 32 * r, 1), rolled)
            pairs = jnp.where(odd4 == 1, pltpu.roll(second, 64, 1), second)
            src[i * 9 + k, 0:4] = jnp.where(even, pltpu.roll(last, 64, 1), low)
            src[i * 9 + k, 4:5] = jnp.sum(jnp.where(ends3, rolled, 0.0), axis=0, keepdims=True)
            src[i * 9 + k, 5:6] = jnp.sum(jnp.where(ends2 & (row4 < 2), pairs, 0.0), axis=0, keepdims=True)
            src[i * 9 + k, 6:7] = jnp.sum(jnp.where(ends2 & (row4 >= 2), pairs, 0.0), axis=0, keepdims=True)
        return carry

    def build(i, carry):
        for k in range(9):
            for r in range(7):
                taps_row = jnp.broadcast_to(src[i * 9 + k, r : r + 1, :], (32, 128))
                skewed = pltpu.roll(taps_row, 0, 1, stride=1, stride_axis=0)
                keep = keep1 if r < 4 else (keep3 if r == 4 else keep2)
                band[i, 32 * k : 32 * k + 32, 128 * r : 128 * r + 128] = jnp.where(keep >= 0, skewed, 0.0).astype(BF16)
        return carry

    lax.fori_loop(0, 8, sources, 0)
    lax.fori_loop(0, 8, build, 0)

    def at(x):
        return pl.multiple_of(x, 32)

    halves = (
        (at(96 * (1 - h)), at(64 + 32 * h), at(32 + 96 * h), at(32 * (1 - h))),
        (at(64 - 32 * h), at(32 + 96 * h), at(160 * h), at(32 * h)),
    )

    def piece(layer, i, x, width, c0, cw):
        return f[layer, i : i + 4, pl.ds(x, width), c0 : c0 + cw]

    def first_two(layer, i, half, c0, cw):
        low = piece(layer, i, halves[half][0], 96, c0, cw)
        high = piece(layer, i, halves[half][1], 32, c0, cw)
        return jnp.concatenate([low, high], axis=1).reshape(512, cw)

    def third(layer, i, half, c0, cw):
        return piece(layer, i, halves[half][2], 32, c0, cw).reshape(128, cw)

    def whole(layer, i, half, c0, cw):
        return jnp.concatenate([first_two(layer, i, half, c0, cw), third(layer, i, half, c0, cw)], axis=0)

    def nearby(layer, i, half, c0, cw):
        if half == 0:
            return first_two(layer, i, half, c0, cw)
        low = piece(layer, i, halves[1][0], 96, c0, cw)
        return jnp.concatenate([low, jnp.zeros((4, 32, cw), BF16)], axis=1).reshape(512, cw)

    def mixed(layer, r, columns):
        def weights(k):
            return jnp.concatenate([mixf[layer, k : k + 1, lo:hi] for lo, hi in columns], axis=1)

        total = r[0:32] * weights(0)
        for k in range(1, 9):
            total += r[32 * k : 32 * k + 32] * weights(k)
        return total

    def put(i, half, c0, cw, total):
        rows = pl.ds(pl.multiple_of(i * 64 + halves[half][3], 32), 32)
        act[rows, c0 : c0 + cw] = gelu(total).astype(BF16)

    def tiles(layer, i, lanes, operand, emit):
        for half in range(2):
            for c0 in (0, 256):
                r = jnp.dot(band[i, :, 0:lanes], operand(layer, i, half, c0, 256), preferred_element_type=F32)
                emit(i, half, c0, 256, mixed(layer, r, ((c0, c0 + 256),)))
        both = jnp.concatenate([operand(layer, i, half, 512, 128) for half in range(2)], axis=1)
        r = jnp.dot(band[i, :, 0:lanes], both, preferred_element_type=F32)
        total = mixed(layer, r, ((512, 640), (512, 640)))
        for half in range(2):
            emit(i, half, 512, 128, total[:, 128 * half : 128 * half + 128])

    def conv(layer, *lats):
        for i in lats:
            tiles(layer, i, 640, whole, put)

    def near(layer, *lats):
        def keep(i, half, c0, cw, total):
            part[i, 32 * half : 32 * half + 32, c0 : c0 + cw] = total

        for i in lats:
            tiles(layer, i, 512, nearby, keep)

    def far(layer, *lats):
        for i in lats:
            for c0, cw in ((0, 256), (256, 256), (512, 128)):
                side = f[layer, i : i + 4, chip_side, c0 : c0 + cw].reshape(256, cw)
                for half, columns, operand in (
                    (0, slice(512, 640), third(layer, i, 0, c0, cw)),
                    (1, slice(640, 896), side),
                ):
                    r = jnp.dot(band[i, :, columns], operand, preferred_element_type=F32)
                    before = part[i, 32 * half : 32 * half + 32, c0 : c0 + cw]
                    put(i, half, c0, cw, before + mixed(layer, r, ((c0, c0 + cw),)))

    def store(row, rows):
        return pltpu.make_async_copy(res.at[pl.ds(row, rows)], out.at[pl.ds(row, rows)], store_sem.at[row // 2])

    def mlp(layer, row, rows):
        hidden = jnp.dot(act[row * 64 : (row + rows) * 64], w1[layer], preferred_element_type=F32)
        hidden = gelu(hidden).astype(BF16)
        update = jnp.dot(hidden, w2[layer], preferred_element_type=F32)
        field = f[layer, row + 2 : row + 2 + rows, own, :].astype(F32)
        result = (field + update.reshape(rows, 64, 640)).astype(BF16)
        if layer == 0:
            f[1, row + 2 : row + 2 + rows, own, :] = result
        else:
            res[row : row + rows] = result
            store(row, rows).start()

    local["in1"].start()
    local["out1"].start()
    arrived(0, "p6", "p4", "p2")
    near(0, 6, 5, 4)
    arrived(0, "p0")
    near(0, 3, 2)
    arrived(0, "up")
    begin(0, "fup")
    arrived(0, "z6")
    begin(0, "sdown")
    arrived(0, "down")
    begin(0, "fdown")
    arrived(0, "z4")
    far(0, 6)
    arrived(0, "sup", "fup")
    conv(0, 7)
    local["in0"].wait()
    local["out0"].wait()
    mlp(0, 6, 2)
    begin(1, "z6", "down", "p6")
    arrived(0, "z2")
    far(0, 4, 5)
    mlp(0, 4, 2)
    begin(1, "z4", "p4")
    arrived(0, "z0", "z1")
    far(0, 2, 3)
    mlp(0, 2, 2)
    begin(1, "z2", "p2")
    arrived(0, "sdown", "fdown")
    conv(0, 0, 1)
    arrived(1, "z6")
    begin(1, "sdown")
    mlp(0, 0, 2)
    begin(1, "z0", "up", "p0", "z1")

    arrived(1, "p4", "p6", "z4")
    conv(1, 6)
    arrived(1, "p2")
    near(1, 5, 4)
    arrived(1, "z2")
    far(1, 4, 5)
    arrived(1, "down")
    begin(1, "fdown")
    arrived(1, "z0")
    begin(1, "sup")
    arrived(1, "up")
    begin(1, "fup")
    local["in1"].wait()
    local["out1"].wait()
    mlp(1, 4, 2)
    arrived(1, "p0", "z1")
    conv(1, 2, 3)
    arrived(1, "sdown", "fdown")
    conv(1, 0, 1)
    mlp(1, 0, 4)
    arrived(1, "sup", "fup")
    conv(1, 7)
    mlp(1, 6, 2)

    for row, rows in ((4, 2), (0, 4), (6, 2)):
        store(row, rows).wait()
    for layer in range(2):
        for name in NAMES:
            act_on(layer, name, "sent")


def shards(n_polar, n_azimuth, grid, taps, start, count, mix, w_in, w_out):
    copies = 2 * len(NAMES)
    hbm = pl.BlockSpec(memory_space=pl.ANY)
    return pl.pallas_call(
        functools.partial(body, n_polar, n_azimuth),
        out_shape=jax.ShapeDtypeStruct(grid.shape, grid.dtype),
        in_specs=[hbm] * 7,
        out_specs=hbm,
        scratch_shapes=[
            pltpu.VMEM((2, 11, 192, 640), BF16),
            pltpu.VMEM((8, 288, 896), BF16),
            pltpu.VMEM(w_in.shape, BF16),
            pltpu.VMEM(w_out.shape, BF16),
            pltpu.VMEM(taps.shape, BF16),
            pltpu.SMEM(start.shape, jnp.int32),
            pltpu.SMEM(count.shape, jnp.int32),
            pltpu.VMEM((9, 2, 640), BF16),
            pltpu.VMEM((72, 8, 128), F32),
            pltpu.VMEM((512, 640), BF16),
            pltpu.VMEM((2, 16, 640), F32),
            pltpu.VMEM(grid.shape, BF16),
            pltpu.VMEM(grid.shape, F32),
            pltpu.SemaphoreType.DMA((copies,)),
            pltpu.SemaphoreType.DMA((copies,)),
            pltpu.SemaphoreType.DMA((9,)),
            pltpu.SemaphoreType.DMA((4,)),
        ],
        compiler_params=pltpu.CompilerParams(
            collective_id=0, has_side_effects=True, vmem_limit_bytes=60 * 2**20
        ),
    )(grid, taps, start, count, jnp.transpose(mix, (1, 0, 2)), w_in, w_out)


def solution(mesh):
    return jax.shard_map(
        functools.partial(shards, mesh.shape["polar"], mesh.shape["azimuth"]),
        mesh=mesh,
        in_specs=(
            P("polar", "azimuth", None),
            P("polar", None, None, None),
            P("polar"),
            P("polar"),
            P(),
            P(),
            P(),
        ),
        out_specs=P("polar", "azimuth", None),
        check_vma=False,
    )
```

```python
import functools

import jax
import jax.numpy as jnp
from jax import lax
from jax.experimental import pallas as pl
from jax.experimental.pallas import tpu as pltpu
from jax.sharding import PartitionSpec as P

F32 = jnp.float32
BF16 = jnp.bfloat16
MESH = pl.DeviceIdType.MESH
NAMES = (
    "z0", "z1", "z2", "z4", "z6", "p0", "p2", "p4", "p6",
    "down", "up", "sdown", "sup", "fdown", "fup",
)


def gelu(x):
    return 0.5 * x * (1.0 + lax.erf(x * 0.7071067811865476))


def body(
    n_polar, n_azimuth,
    grid, taps_in, start_in, count_in, mix_in, w_in, w_out, out,
    f, band, w1, w2, taps, start, count, mix, src, act, mixf, res, part,
    send_sem, recv_sem, local_sem, store_sem,
):
    p = lax.axis_index("polar")
    a = lax.axis_index("azimuth")
    h = lax.rem(a, 2)
    pair = a + 1 - 2 * h
    zside = lax.rem(a + n_azimuth - 1 + 2 * h, n_azimuth)
    has_low = p > 0
    has_high = p < n_polar - 1
    own = pl.ds(64, 64)
    core_side = pl.ds(pl.multiple_of(128 * (1 - h), 128), 64)
    chip_side = pl.ds(pl.multiple_of(128 * h, 128), 64)

    barrier = pltpu.get_barrier_semaphore()
    for peer in (pair, zside):
        pl.semaphore_signal(barrier, inc=1, device_id=(p, peer), device_id_type=MESH)

    @pl.when(has_low)
    def _():
        pl.semaphore_signal(barrier, inc=1, device_id=(p - 1, a), device_id_type=MESH)

    @pl.when(has_high)
    def _():
        pl.semaphore_signal(barrier, inc=1, device_id=(p + 1, a), device_id_type=MESH)

    def field_rows(layer, row, rows):
        return f.at[layer, pl.ds(row + 2, rows), own]

    def transfer(layer, name):
        if name[0] == "z":
            row = int(name[1])
            rows = 1 if row < 2 else 2
            return (field_rows(layer, row, rows), f.at[layer, pl.ds(row + 2, rows), core_side], (p, zside), None, None)
        if name[0] == "p":
            row = int(name[1])
            return (field_rows(layer, row, 2), f.at[layer, pl.ds(row + 2, 2), chip_side], (p, pair), None, None)
        if name == "down":
            return (field_rows(layer, 6, 2), f.at[layer, pl.ds(0, 2), own], (p + 1, a), has_high, has_low)
        if name == "up":
            return (field_rows(layer, 0, 1), f.at[layer, pl.ds(10, 1), own], (p - 1, a), has_low, has_high)
        if name == "sdown":
            return (f.at[layer, pl.ds(8, 2), chip_side], f.at[layer, pl.ds(0, 2), chip_side], (p + 1, a), has_high, has_low)
        if name == "sup":
            return (f.at[layer, pl.ds(2, 1), chip_side], f.at[layer, pl.ds(10, 1), chip_side], (p - 1, a), has_low, has_high)
        if name == "fdown":
            return (f.at[layer, pl.ds(0, 2), own], f.at[layer, pl.ds(0, 2), chip_side], (p, pair), has_low, has_low)
        return (f.at[layer, pl.ds(10, 1), own], f.at[layer, pl.ds(10, 1), chip_side], (p, pair), has_high, has_high)

    def act_on(layer, name, what):
        source, target, device, sends, receives = transfer(layer, name)
        number = layer * len(NAMES) + NAMES.index(name)
        copy = pltpu.make_async_remote_copy(
            src_ref=source, dst_ref=target, send_sem=send_sem.at[number],
            recv_sem=recv_sem.at[number], device_id=device, device_id_type=MESH,
        )
        run = {"start": copy.start, "recv": copy.wait_recv, "sent": copy.wait_send}[what]
        when = receives if what == "recv" else sends
        if when is None:
            run()
        else:
            pl.when(when)(run)

    def begin(layer, *names):
        for name in names:
            act_on(layer, name, "start")

    def arrived(layer, *names):
        for name in names:
            act_on(layer, name, "recv")

    local = {
        name: pltpu.make_async_copy(source, target, local_sem.at[number])
        for number, (name, source, target) in enumerate((
            ("taps", taps_in, taps),
            ("start", start_in, start),
            ("count", count_in, count),
            ("mix", mix_in, mix),
            ("field", grid, f.at[0, pl.ds(2, 8), own]),
            ("in0", w_in.at[0], w1.at[0]),
            ("out0", w_out.at[0], w2.at[0]),
            ("in1", w_in.at[1], w1.at[1]),
            ("out1", w_out.at[1], w2.at[1]),
        ))
    }
    for name in ("field", "taps", "start", "count", "mix"):
        local[name].start()
    local["field"].wait()

    pl.semaphore_wait(barrier, 2 + has_low.astype(jnp.int32) + has_high.astype(jnp.int32))

    begin(0, "z0", "up", "z6", "down", "z4", "p6", "p4", "z2", "p2", "p0", "z1")
    local["in0"].start()
    local["out0"].start()

    @pl.when(p == 0)
    def _():
        for layer in range(2):
            f[layer, 0:2] = jnp.zeros((2, 192, 640), BF16)

    @pl.when(p == n_polar - 1)
    def _():
        for layer in range(2):
            f[layer, 10:11] = jnp.zeros((1, 192, 640), BF16)

    for name in ("taps", "start", "count", "mix"):
        local[name].wait()
    for layer in range(2):
        for k in range(9):
            mixf[layer, k : k + 1] = mix[k, layer : layer + 1].astype(F32)

    even = h == 0
    offset = lax.broadcasted_iota(jnp.int32, (4, 129), 1) - 64
    lane4 = lax.broadcasted_iota(jnp.int32, (4, 128), 1)
    row4 = lax.broadcasted_iota(jnp.int32, (4, 128), 0)
    odd4 = row4 & 1
    lane = lax.broadcasted_iota(jnp.int32, (32, 128), 1)
    row = lax.broadcasted_iota(jnp.int32, (32, 128), 0)
    ends3 = ((lane4 - 97 * h - 32 * row4) & 127) < 32
    ends2 = ((lane4 - 97 * h - 64 * odd4) & 127) < 64
    keep1 = jnp.where(even, jnp.where(lane >= 96, 0, 64 + row - lane), lane - row)
    keep3 = jnp.where(even, (lane & 31) - row, row - (lane & 31))
    keep2 = jnp.where(even, (lane & 63) - row, 32 + row - (lane & 63))

    def sources(i, carry):
        inside = (offset >= start[i]) & (offset < start[i] + count[i])
        for k in range(9):
            v = jnp.where(inside, taps[i, k].astype(F32), 0.0)
            low = v[:, 0:128]
            last = jnp.where(lane4 == 0, jnp.broadcast_to(v[:, 128:129], (4, 128)), low)
            third = jnp.where(even, low, last)
            second = jnp.where(even, low, pltpu.roll(last, 32, 1))
            rolled = third
            for r in range(1, 4):
                rolled = jnp.where(row4 == r, pltpu.roll(third, 32 * r, 1), rolled)
            pairs = jnp.where(odd4 == 1, pltpu.roll(second, 64, 1), second)
            src[i * 9 + k, 0:4] = jnp.where(even, pltpu.roll(last, 64, 1), low)
            src[i * 9 + k, 4:5] = jnp.sum(jnp.where(ends3, rolled, 0.0), axis=0, keepdims=True)
            src[i * 9 + k, 5:6] = jnp.sum(jnp.where(ends2 & (row4 < 2), pairs, 0.0), axis=0, keepdims=True)
            src[i * 9 + k, 6:7] = jnp.sum(jnp.where(ends2 & (row4 >= 2), pairs, 0.0), axis=0, keepdims=True)
        return carry

    def build(i, carry):
        for k in range(9):
            for r in range(7):
                taps_row = jnp.broadcast_to(src[i * 9 + k, r : r + 1, :], (32, 128))
                skewed = pltpu.roll(taps_row, 0, 1, stride=1, stride_axis=0)
                keep = keep1 if r < 4 else (keep3 if r == 4 else keep2)
                band[i, 32 * k : 32 * k + 32, 128 * r : 128 * r + 128] = jnp.where(keep >= 0, skewed, 0.0).astype(BF16)
        return carry

    lax.fori_loop(0, 8, sources, 0)
    lax.fori_loop(0, 8, build, 0)

    def at(x):
        return pl.multiple_of(x, 32)

    halves = (
        (at(96 * (1 - h)), at(64 + 32 * h), at(32 + 96 * h), at(32 * (1 - h))),
        (at(64 - 32 * h), at(32 + 96 * h), at(160 * h), at(32 * h)),
    )

    def piece(layer, i, x, width, c0, cw):
        return f[layer, i : i + 4, pl.ds(x, width), c0 : c0 + cw]

    def first_two(layer, i, half, c0, cw):
        low = piece(layer, i, halves[half][0], 96, c0, cw)
        high = piece(layer, i, halves[half][1], 32, c0, cw)
        return jnp.concatenate([low, high], axis=1).reshape(512, cw)

    def third(layer, i, half, c0, cw):
        return piece(layer, i, halves[half][2], 32, c0, cw).reshape(128, cw)

    def whole(layer, i, half, c0, cw):
        return jnp.concatenate([first_two(layer, i, half, c0, cw), third(layer, i, half, c0, cw)], axis=0)

    def nearby(layer, i, half, c0, cw):
        if half == 0:
            return first_two(layer, i, half, c0, cw)
        low = piece(layer, i, halves[1][0], 96, c0, cw)
        return jnp.concatenate([low, jnp.zeros((4, 32, cw), BF16)], axis=1).reshape(512, cw)

    def mixed(layer, r, columns):
        def weights(k):
            return jnp.concatenate([mixf[layer, k : k + 1, lo:hi] for lo, hi in columns], axis=1)

        total = r[0:32] * weights(0)
        for k in range(1, 9):
            total += r[32 * k : 32 * k + 32] * weights(k)
        return total

    def put(i, half, c0, cw, total):
        rows = pl.ds(pl.multiple_of(i * 64 + halves[half][3], 32), 32)
        act[rows, c0 : c0 + cw] = gelu(total).astype(BF16)

    def tiles(layer, i, lanes, operand, emit):
        for half in range(2):
            for c0 in (0, 256):
                r = jnp.dot(band[i, :, 0:lanes], operand(layer, i, half, c0, 256), preferred_element_type=F32)
                emit(i, half, c0, 256, mixed(layer, r, ((c0, c0 + 256),)))
        both = jnp.concatenate([operand(layer, i, half, 512, 128) for half in range(2)], axis=1)
        r = jnp.dot(band[i, :, 0:lanes], both, preferred_element_type=F32)
        total = mixed(layer, r, ((512, 640), (512, 640)))
        for half in range(2):
            emit(i, half, 512, 128, total[:, 128 * half : 128 * half + 128])

    def conv(layer, *lats):
        for i in lats:
            tiles(layer, i, 640, whole, put)

    def near(layer, *lats):
        def keep(i, half, c0, cw, total):
            part[i, 32 * half : 32 * half + 32, c0 : c0 + cw] = total

        for i in lats:
            tiles(layer, i, 512, nearby, keep)

    def far(layer, *lats):
        for i in lats:
            for c0, cw in ((0, 256), (256, 256), (512, 128)):
                side = f[layer, i : i + 4, chip_side, c0 : c0 + cw].reshape(256, cw)
                for half, columns, operand in (
                    (0, slice(512, 640), third(layer, i, 0, c0, cw)),
                    (1, slice(640, 896), side),
                ):
                    r = jnp.dot(band[i, :, columns], operand, preferred_element_type=F32)
                    before = part[i, 32 * half : 32 * half + 32, c0 : c0 + cw]
                    put(i, half, c0, cw, before + mixed(layer, r, ((c0, c0 + cw),)))

    def store(row, rows):
        return pltpu.make_async_copy(res.at[pl.ds(row, rows)], out.at[pl.ds(row, rows)], store_sem.at[row // 2])

    def mlp(layer, row, rows):
        hidden = jnp.dot(act[row * 64 : (row + rows) * 64], w1[layer], preferred_element_type=F32)
        hidden = gelu(hidden).astype(BF16)
        update = jnp.dot(hidden, w2[layer], preferred_element_type=F32)
        field = f[layer, row + 2 : row + 2 + rows, own, :].astype(F32)
        result = (field + update.reshape(rows, 64, 640)).astype(BF16)
        if layer == 0:
            f[1, row + 2 : row + 2 + rows, own, :] = result
        else:
            res[row : row + rows] = result
            store(row, rows).start()

    local["in1"].start()
    local["out1"].start()
    arrived(0, "p6", "p4", "p2")
    near(0, 6, 5, 4)
    arrived(0, "z0")
    begin(0, "sup")
    arrived(0, "up")
    begin(0, "fup")
    arrived(0, "p0")
    near(0, 3, 2)
    arrived(0, "z6")
    begin(0, "sdown")
    arrived(0, "down")
    begin(0, "fdown")
    arrived(0, "z4")
    far(0, 6)
    arrived(0, "sup", "fup")
    conv(0, 7)
    local["in0"].wait()
    local["out0"].wait()
    mlp(0, 6, 2)
    begin(1, "z6", "down", "p6")
    arrived(0, "z2")
    far(0, 4, 5)
    mlp(0, 4, 2)
    begin(1, "z4", "p4")
    arrived(0, "z1")
    far(0, 2, 3)
    mlp(0, 2, 2)
    begin(1, "z2", "p2")
    arrived(0, "sdown", "fdown")
    conv(0, 0, 1)
    arrived(1, "z6")
    begin(1, "sdown")
    mlp(0, 0, 2)
    begin(1, "z0", "up", "p0", "z1")

    arrived(1, "p4", "p6", "z4")
    conv(1, 6)
    arrived(1, "p2")
    near(1, 5, 4)
    arrived(1, "z2")
    far(1, 4, 5)
    arrived(1, "down")
    begin(1, "fdown")
    arrived(1, "z0")
    begin(1, "sup")
    arrived(1, "up")
    begin(1, "fup")
    local["in1"].wait()
    local["out1"].wait()
    mlp(1, 4, 2)
    arrived(1, "p0", "z1")
    conv(1, 2, 3)
    arrived(1, "sdown", "fdown")
    conv(1, 0, 1)
    mlp(1, 0, 4)
    arrived(1, "sup", "fup")
    conv(1, 7)
    mlp(1, 6, 2)

    for row, rows in ((4, 2), (0, 4), (6, 2)):
        store(row, rows).wait()
    for layer in range(2):
        for name in NAMES:
            act_on(layer, name, "sent")


def shards(n_polar, n_azimuth, grid, taps, start, count, mix, w_in, w_out):
    copies = 2 * len(NAMES)
    hbm = pl.BlockSpec(memory_space=pl.ANY)
    return pl.pallas_call(
        functools.partial(body, n_polar, n_azimuth),
        out_shape=jax.ShapeDtypeStruct(grid.shape, grid.dtype),
        in_specs=[hbm] * 7,
        out_specs=hbm,
        scratch_shapes=[
            pltpu.VMEM((2, 11, 192, 640), BF16),
            pltpu.VMEM((8, 288, 896), BF16),
            pltpu.VMEM(w_in.shape, BF16),
            pltpu.VMEM(w_out.shape, BF16),
            pltpu.VMEM(taps.shape, BF16),
            pltpu.SMEM(start.shape, jnp.int32),
            pltpu.SMEM(count.shape, jnp.int32),
            pltpu.VMEM((9, 2, 640), BF16),
            pltpu.VMEM((72, 8, 128), F32),
            pltpu.VMEM((512, 640), BF16),
            pltpu.VMEM((2, 16, 640), F32),
            pltpu.VMEM(grid.shape, BF16),
            pltpu.VMEM(grid.shape, F32),
            pltpu.SemaphoreType.DMA((copies,)),
            pltpu.SemaphoreType.DMA((copies,)),
            pltpu.SemaphoreType.DMA((9,)),
            pltpu.SemaphoreType.DMA((4,)),
        ],
        compiler_params=pltpu.CompilerParams(
            collective_id=0, has_side_effects=True, vmem_limit_bytes=60 * 2**20
        ),
    )(grid, taps, start, count, jnp.transpose(mix, (1, 0, 2)), w_in, w_out)


def solution(mesh):
    return jax.shard_map(
        functools.partial(shards, mesh.shape["polar"], mesh.shape["azimuth"]),
        mesh=mesh,
        in_specs=(
            P("polar", "azimuth", None),
            P("polar", None, None, None),
            P("polar"),
            P("polar"),
            P(),
            P(),
            P(),
        ),
        out_specs=P("polar", "azimuth", None),
        check_vma=False,
    )
```

```python
import functools

import jax
import jax.numpy as jnp
from jax import lax
from jax.experimental import pallas as pl
from jax.experimental.pallas import tpu as pltpu
from jax.sharding import PartitionSpec as P

F32 = jnp.float32
BF16 = jnp.bfloat16
MESH = pl.DeviceIdType.MESH
NAMES = (
    "z0", "z1", "z2", "z4", "z6", "p0", "p2", "p4", "p6",
    "down", "up", "sdown", "sup", "fdown", "fup",
)


def gelu(x):
    return 0.5 * x * (1.0 + lax.erf(x * 0.7071067811865476))


def body(
    n_polar, n_azimuth,
    grid, taps_in, start_in, count_in, mix_in, w_in, w_out, out,
    f, band, w1, w2, taps, start, count, mix, src, act, mixf, res, part,
    send_sem, recv_sem, local_sem, store_sem,
):
    p = lax.axis_index("polar")
    a = lax.axis_index("azimuth")
    h = lax.rem(a, 2)
    pair = a + 1 - 2 * h
    zside = lax.rem(a + n_azimuth - 1 + 2 * h, n_azimuth)
    has_low = p > 0
    has_high = p < n_polar - 1
    own = pl.ds(64, 64)
    core_side = pl.ds(pl.multiple_of(128 * (1 - h), 128), 64)
    chip_side = pl.ds(pl.multiple_of(128 * h, 128), 64)

    barrier = pltpu.get_barrier_semaphore()
    for peer in (pair, zside):
        pl.semaphore_signal(barrier, inc=1, device_id=(p, peer), device_id_type=MESH)

    @pl.when(has_low)
    def _():
        pl.semaphore_signal(barrier, inc=1, device_id=(p - 1, a), device_id_type=MESH)

    @pl.when(has_high)
    def _():
        pl.semaphore_signal(barrier, inc=1, device_id=(p + 1, a), device_id_type=MESH)

    def field_rows(layer, row, rows):
        return f.at[layer, pl.ds(row + 2, rows), own]

    def transfer(layer, name):
        if name[0] == "z":
            row = int(name[1])
            rows = 1 if row < 2 else 2
            return (field_rows(layer, row, rows), f.at[layer, pl.ds(row + 2, rows), core_side], (p, zside), None, None)
        if name[0] == "p":
            row = int(name[1])
            return (field_rows(layer, row, 2), f.at[layer, pl.ds(row + 2, 2), chip_side], (p, pair), None, None)
        if name == "down":
            return (field_rows(layer, 6, 2), f.at[layer, pl.ds(0, 2), own], (p + 1, a), has_high, has_low)
        if name == "up":
            return (field_rows(layer, 0, 1), f.at[layer, pl.ds(10, 1), own], (p - 1, a), has_low, has_high)
        if name == "sdown":
            return (f.at[layer, pl.ds(8, 2), chip_side], f.at[layer, pl.ds(0, 2), chip_side], (p + 1, a), has_high, has_low)
        if name == "sup":
            return (f.at[layer, pl.ds(2, 1), chip_side], f.at[layer, pl.ds(10, 1), chip_side], (p - 1, a), has_low, has_high)
        if name == "fdown":
            return (f.at[layer, pl.ds(0, 2), own], f.at[layer, pl.ds(0, 2), chip_side], (p, pair), has_low, has_low)
        return (f.at[layer, pl.ds(10, 1), own], f.at[layer, pl.ds(10, 1), chip_side], (p, pair), has_high, has_high)

    def act_on(layer, name, what):
        source, target, device, sends, receives = transfer(layer, name)
        number = layer * len(NAMES) + NAMES.index(name)
        copy = pltpu.make_async_remote_copy(
            src_ref=source, dst_ref=target, send_sem=send_sem.at[number],
            recv_sem=recv_sem.at[number], device_id=device, device_id_type=MESH,
        )
        run = {"start": copy.start, "recv": copy.wait_recv, "sent": copy.wait_send}[what]
        when = receives if what == "recv" else sends
        if when is None:
            run()
        else:
            pl.when(when)(run)

    def begin(layer, *names):
        for name in names:
            act_on(layer, name, "start")

    def arrived(layer, *names):
        for name in names:
            act_on(layer, name, "recv")

    local = {
        name: pltpu.make_async_copy(source, target, local_sem.at[number])
        for number, (name, source, target) in enumerate((
            ("taps", taps_in, taps),
            ("start", start_in, start),
            ("count", count_in, count),
            ("mix", mix_in, mix),
            ("field", grid, f.at[0, pl.ds(2, 8), own]),
            ("in0", w_in.at[0], w1.at[0]),
            ("out0", w_out.at[0], w2.at[0]),
            ("in1", w_in.at[1], w1.at[1]),
            ("out1", w_out.at[1], w2.at[1]),
        ))
    }
    for name in ("field", "taps", "start", "count", "mix"):
        local[name].start()
    local["field"].wait()

    pl.semaphore_wait(barrier, 2 + has_low.astype(jnp.int32) + has_high.astype(jnp.int32))

    begin(0, "z0", "up", "z6", "down", "z4", "p6", "p4", "z2", "p2", "p0", "z1")
    local["in0"].start()
    local["out0"].start()

    @pl.when(p == 0)
    def _():
        for layer in range(2):
            f[layer, 0:2] = jnp.zeros((2, 192, 640), BF16)

    @pl.when(p == n_polar - 1)
    def _():
        for layer in range(2):
            f[layer, 10:11] = jnp.zeros((1, 192, 640), BF16)

    for name in ("taps", "start", "count", "mix"):
        local[name].wait()
    for layer in range(2):
        for k in range(9):
            mixf[layer, k : k + 1] = mix[k, layer : layer + 1].astype(F32)

    even = h == 0
    offset = lax.broadcasted_iota(jnp.int32, (4, 129), 1) - 64
    lane4 = lax.broadcasted_iota(jnp.int32, (4, 128), 1)
    row4 = lax.broadcasted_iota(jnp.int32, (4, 128), 0)
    odd4 = row4 & 1
    lane = lax.broadcasted_iota(jnp.int32, (32, 128), 1)
    row = lax.broadcasted_iota(jnp.int32, (32, 128), 0)
    ends3 = ((lane4 - 97 * h - 32 * row4) & 127) < 32
    ends2 = ((lane4 - 97 * h - 64 * odd4) & 127) < 64
    keep1 = jnp.where(even, jnp.where(lane >= 96, 0, 64 + row - lane), lane - row)
    keep3 = jnp.where(even, (lane & 31) - row, row - (lane & 31))
    keep2 = jnp.where(even, (lane & 63) - row, 32 + row - (lane & 63))

    def sources(i, carry):
        inside = (offset >= start[i]) & (offset < start[i] + count[i])
        for k in range(9):
            v = jnp.where(inside, taps[i, k].astype(F32), 0.0)
            low = v[:, 0:128]
            last = jnp.where(lane4 == 0, jnp.broadcast_to(v[:, 128:129], (4, 128)), low)
            third = jnp.where(even, low, last)
            second = jnp.where(even, low, pltpu.roll(last, 32, 1))
            rolled = third
            for r in range(1, 4):
                rolled = jnp.where(row4 == r, pltpu.roll(third, 32 * r, 1), rolled)
            pairs = jnp.where(odd4 == 1, pltpu.roll(second, 64, 1), second)
            src[i * 9 + k, 0:4] = jnp.where(even, pltpu.roll(last, 64, 1), low)
            src[i * 9 + k, 4:5] = jnp.sum(jnp.where(ends3, rolled, 0.0), axis=0, keepdims=True)
            src[i * 9 + k, 5:6] = jnp.sum(jnp.where(ends2 & (row4 < 2), pairs, 0.0), axis=0, keepdims=True)
            src[i * 9 + k, 6:7] = jnp.sum(jnp.where(ends2 & (row4 >= 2), pairs, 0.0), axis=0, keepdims=True)
        return carry

    def build(i, carry):
        for k in range(9):
            for r in range(7):
                taps_row = jnp.broadcast_to(src[i * 9 + k, r : r + 1, :], (32, 128))
                skewed = pltpu.roll(taps_row, 0, 1, stride=1, stride_axis=0)
                keep = keep1 if r < 4 else (keep3 if r == 4 else keep2)
                band[i, 32 * k : 32 * k + 32, 128 * r : 128 * r + 128] = jnp.where(keep >= 0, skewed, 0.0).astype(BF16)
        return carry

    lax.fori_loop(0, 8, sources, 0)
    lax.fori_loop(0, 8, build, 0)

    def at(x):
        return pl.multiple_of(x, 32)

    halves = (
        (at(96 * (1 - h)), at(64 + 32 * h), at(32 + 96 * h), at(32 * (1 - h))),
        (at(64 - 32 * h), at(32 + 96 * h), at(160 * h), at(32 * h)),
    )

    def piece(layer, i, x, width, c0, cw):
        return f[layer, i : i + 4, pl.ds(x, width), c0 : c0 + cw]

    def first_two(layer, i, half, c0, cw):
        low = piece(layer, i, halves[half][0], 96, c0, cw)
        high = piece(layer, i, halves[half][1], 32, c0, cw)
        return jnp.concatenate([low, high], axis=1).reshape(512, cw)

    def third(layer, i, half, c0, cw):
        return piece(layer, i, halves[half][2], 32, c0, cw).reshape(128, cw)

    def whole(layer, i, half, c0, cw):
        return jnp.concatenate([first_two(layer, i, half, c0, cw), third(layer, i, half, c0, cw)], axis=0)

    def nearby(layer, i, half, c0, cw):
        if half == 0:
            return first_two(layer, i, half, c0, cw)
        low = piece(layer, i, halves[1][0], 96, c0, cw)
        return jnp.concatenate([low, jnp.zeros((4, 32, cw), BF16)], axis=1).reshape(512, cw)

    def mixed(layer, r, columns):
        def weights(k):
            return jnp.concatenate([mixf[layer, k : k + 1, lo:hi] for lo, hi in columns], axis=1)

        total = r[0:32] * weights(0)
        for k in range(1, 9):
            total += r[32 * k : 32 * k + 32] * weights(k)
        return total

    def put(i, half, c0, cw, total):
        rows = pl.ds(pl.multiple_of(i * 64 + halves[half][3], 32), 32)
        act[rows, c0 : c0 + cw] = gelu(total).astype(BF16)

    def tiles(layer, i, lanes, operand, emit):
        for half in range(2):
            for c0 in (0, 256):
                r = jnp.dot(band[i, :, 0:lanes], operand(layer, i, half, c0, 256), preferred_element_type=F32)
                emit(i, half, c0, 256, mixed(layer, r, ((c0, c0 + 256),)))
        both = jnp.concatenate([operand(layer, i, half, 512, 128) for half in range(2)], axis=1)
        r = jnp.dot(band[i, :, 0:lanes], both, preferred_element_type=F32)
        total = mixed(layer, r, ((512, 640), (512, 640)))
        for half in range(2):
            emit(i, half, 512, 128, total[:, 128 * half : 128 * half + 128])

    def conv(layer, *lats):
        for i in lats:
            tiles(layer, i, 640, whole, put)

    def near(layer, *lats):
        def keep(i, half, c0, cw, total):
            part[i, 32 * half : 32 * half + 32, c0 : c0 + cw] = total

        for i in lats:
            tiles(layer, i, 512, nearby, keep)

    def far(layer, *lats):
        for i in lats:
            for c0, cw in ((0, 256), (256, 256), (512, 128)):
                side = f[layer, i : i + 4, chip_side, c0 : c0 + cw].reshape(256, cw)
                for half, columns, operand in (
                    (0, slice(512, 640), third(layer, i, 0, c0, cw)),
                    (1, slice(640, 896), side),
                ):
                    r = jnp.dot(band[i, :, columns], operand, preferred_element_type=F32)
                    before = part[i, 32 * half : 32 * half + 32, c0 : c0 + cw]
                    put(i, half, c0, cw, before + mixed(layer, r, ((c0, c0 + cw),)))

    def store(row, rows):
        return pltpu.make_async_copy(res.at[pl.ds(row, rows)], out.at[pl.ds(row, rows)], store_sem.at[row // 2])

    def mlp(layer, row, rows):
        hidden = jnp.dot(act[row * 64 : (row + rows) * 64], w1[layer], preferred_element_type=F32)
        hidden = gelu(hidden).astype(BF16)
        update = jnp.dot(hidden, w2[layer], preferred_element_type=F32)
        field = f[layer, row + 2 : row + 2 + rows, own, :].astype(F32)
        result = (field + update.reshape(rows, 64, 640)).astype(BF16)
        if layer == 0:
            f[1, row + 2 : row + 2 + rows, own, :] = result
        else:
            res[row : row + rows] = result
            store(row, rows).start()

    local["in1"].start()
    local["out1"].start()
    arrived(0, "p6", "p4", "p2")
    near(0, 6, 5, 4)
    arrived(0, "z0")
    begin(0, "sup")
    arrived(0, "up")
    begin(0, "fup")
    arrived(0, "p0")
    near(0, 3, 2)
    arrived(0, "z6")
    begin(0, "sdown")
    arrived(0, "down")
    begin(0, "fdown")
    local["in0"].wait()
    local["out0"].wait()
    arrived(0, "z4", "sup", "fup")
    far(0, 6)
    conv(0, 7)
    mlp(0, 6, 2)
    begin(1, "z6", "down", "p6")
    arrived(0, "z2")
    far(0, 4, 5)
    mlp(0, 4, 2)
    begin(1, "z4", "p4")
    arrived(0, "z1")
    far(0, 2, 3)
    mlp(0, 2, 2)
    begin(1, "z2", "p2")
    arrived(0, "sdown", "fdown")
    conv(0, 0, 1)
    arrived(1, "z6")
    begin(1, "sdown")
    mlp(0, 0, 2)
    begin(1, "z0", "up", "p0", "z1")

    arrived(1, "p4", "p6", "z4")
    conv(1, 6)
    arrived(1, "p2")
    near(1, 5, 4)
    arrived(1, "z2")
    far(1, 4, 5)
    arrived(1, "down")
    begin(1, "fdown")
    arrived(1, "z0")
    begin(1, "sup")
    arrived(1, "up")
    begin(1, "fup")
    local["in1"].wait()
    local["out1"].wait()
    mlp(1, 4, 2)
    arrived(1, "p0", "z1")
    conv(1, 2, 3)
    arrived(1, "sdown", "fdown")
    conv(1, 0, 1)
    mlp(1, 0, 4)
    arrived(1, "sup", "fup")
    conv(1, 7)
    mlp(1, 6, 2)

    for row, rows in ((4, 2), (0, 4), (6, 2)):
        store(row, rows).wait()
    for layer in range(2):
        for name in NAMES:
            act_on(layer, name, "sent")


def shards(n_polar, n_azimuth, grid, taps, start, count, mix, w_in, w_out):
    copies = 2 * len(NAMES)
    hbm = pl.BlockSpec(memory_space=pl.ANY)
    return pl.pallas_call(
        functools.partial(body, n_polar, n_azimuth),
        out_shape=jax.ShapeDtypeStruct(grid.shape, grid.dtype),
        in_specs=[hbm] * 7,
        out_specs=hbm,
        scratch_shapes=[
            pltpu.VMEM((2, 11, 192, 640), BF16),
            pltpu.VMEM((8, 288, 896), BF16),
            pltpu.VMEM(w_in.shape, BF16),
            pltpu.VMEM(w_out.shape, BF16),
            pltpu.VMEM(taps.shape, BF16),
            pltpu.SMEM(start.shape, jnp.int32),
            pltpu.SMEM(count.shape, jnp.int32),
            pltpu.VMEM((9, 2, 640), BF16),
            pltpu.VMEM((72, 8, 128), F32),
            pltpu.VMEM((512, 640), BF16),
            pltpu.VMEM((2, 16, 640), F32),
            pltpu.VMEM(grid.shape, BF16),
            pltpu.VMEM(grid.shape, F32),
            pltpu.SemaphoreType.DMA((copies,)),
            pltpu.SemaphoreType.DMA((copies,)),
            pltpu.SemaphoreType.DMA((9,)),
            pltpu.SemaphoreType.DMA((4,)),
        ],
        compiler_params=pltpu.CompilerParams(
            collective_id=0, has_side_effects=True, vmem_limit_bytes=60 * 2**20
        ),
    )(grid, taps, start, count, jnp.transpose(mix, (1, 0, 2)), w_in, w_out)


def solution(mesh):
    return jax.shard_map(
        functools.partial(shards, mesh.shape["polar"], mesh.shape["azimuth"]),
        mesh=mesh,
        in_specs=(
            P("polar", "azimuth", None),
            P("polar", None, None, None),
            P("polar"),
            P("polar"),
            P(),
            P(),
            P(),
        ),
        out_specs=P("polar", "azimuth", None),
        check_vma=False,
    )
```
